512 devices in a mesh: lon: 16 (over z_hi, y, core), lat: 32 (over z_lo, x).
Axes of the slice: x: 4, y: 4, z: 16 (z_hi: 2, z_lo: 8; z = z_hi * 8 + z_lo), core: 2. Of those that a mesh axis runs over, the one named last changes fastest.
Arguments:
- coarse: bfloat16 [2048, 65536], P('lat', 'lon'), may hold values from -6 to 6
- ocean_mask: int32 [2048], replicated, may hold values from 0 to 1, as said below
- band_plan: int32 [2048], replicated, may hold values from 0 to 31, as said below
- up_weight: bfloat16 [3, 3, 64, 64], replicated, may hold values from -0.75 to 0.75
- up_bias: float32 [64], replicated, may hold values from -3 to 3
- first_weight: bfloat16 [3, 3, 64, 64], replicated, may hold values from -0.25 to 0.25
- first_bias: float32 [64], replicated, may hold values from -3 to 3
- second_weight: bfloat16 [3, 3, 64, 64], replicated, may hold values from -0.25 to 0.25
- second_bias: float32 [64], replicated, may hold values from -3 to 3
- head_weight: bfloat16 [64, 4], replicated, may hold values from -0.75 to 0.75
- head_bias: float32 [4], replicated, may hold values from -3 to 3
Outputs:
- fields: float32 [1024, 3, 12288], P('lat', None, 'lon')
The draws below stay inside these ranges and needn't reach their ends.
Inputs may be any that keep to these rules, and one draw needn't show every extreme that they name: `ocean_mask`: exactly 1024 rows are ocean; the first and the last of the 64 rows of every lat index are ocean; every lat index holds 2 to 62 ocean rows, and some lat index holds exactly 62 of them in every draw. `band_plan`: ocean rows, taken in increasing order, go to the bands in a cyclic order of all 32 bands, so each band receives exactly 32 ocean rows and the rows of one lat index send at most 2 ocean rows to one band, a most that is reached in every draw; a land row holds the band of its own lat index.
All inputs are finite; a program needn't handle non-finite values.
Results may differ from the reference program's by a relative error of at most 0.0075.
Values may be sent and summed in bfloat16 or wider, within the bound.
A program may use at most 64 MiB of HBM per device.

```python
import jax
import jax.numpy as jnp
from jax import lax

C = 64
FIELDS = 4
H = 64
LAT_IN = 2048
LON_IN = 1024
SLOTS = 1024
N_LAT = 32


def ocean_plan(key):
    plan_key = jax.random.fold_in(key, 7)
    key_order, key_lift, key_score, key_turn = jax.random.split(plan_key, 4)
    halfway = N_LAT // 2
    shuffle_order = jax.random.permutation(key_order, N_LAT)
    lift_sizes = jax.random.randint(key_lift, (halfway,), 0, H // 2 - 1).astype(jnp.int32)
    lift_sizes = lift_sizes.at[0].set(H // 2 - 2)
    deltas = jnp.zeros((N_LAT,), jnp.int32)
    deltas = deltas.at[shuffle_order[:halfway]].set(lift_sizes)
    deltas = deltas.at[shuffle_order[halfway:]].set(-lift_sizes)
    counts = H // 2 + deltas
    scores = jax.random.randint(key_score, (N_LAT, H), 0, 1 << 20).astype(jnp.int32) * H + jnp.arange(H, dtype=jnp.int32)[None, :]
    scores = scores.at[:, 0].set(-2).at[:, H - 1].set(-1)
    places = jnp.argsort(jnp.argsort(scores, axis=1, stable=True), axis=1, stable=True)
    ocean_rows = (places < counts[:, None]).astype(jnp.int32).reshape(N_LAT * H)
    band_cycle = jax.random.permutation(key_turn, N_LAT).astype(jnp.int32)
    ranks = jnp.cumsum(ocean_rows) - 1
    homes = jnp.arange(N_LAT * H, dtype=jnp.int32) // H
    band_rows = jnp.where(ocean_rows == 1, band_cycle[jnp.maximum(ranks, 0) % N_LAT], homes)
    return (ocean_rows, band_rows.astype(jnp.int32))


def draw_ocean_mask(key, part):
    return ocean_plan(key)[0]


def draw_band_plan(key, part):
    return ocean_plan(key)[1]


def levels(key, dims, shards, smallest, largest):
    def one(axis_at, blocks):
        heights = jax.random.uniform(jax.random.fold_in(jax.random.fold_in(key, 6), axis_at), (blocks,), jnp.float32, smallest / len(shards), largest / len(shards))
        return jnp.repeat(jnp.exp(heights), dims[axis_at] // blocks).reshape((-1,) + (1,) * (len(dims) - axis_at - 1))

    loudness = one(*shards[0])
    for cut in shards[1:]:
        loudness = loudness * one(*cut)
    return loudness


def scatter_about(own_key, shape, spread, reach, cuts=(), kind=jnp.bfloat16):
    values = spread * jax.random.normal(own_key, shape, jnp.float32)
    if cuts:
        values = values * levels(own_key, shape, cuts, -0.22, 0.18)
    return jnp.clip(values, -reach, reach).astype(kind)


def setup_inputs(seed: int = 0) -> dict:
    keys = jax.random.split(jax.random.key(seed), 12)
    return {
        "coarse": scatter_about(keys[0], (LAT_IN, LON_IN * C), 1.0, 6.0, ((0, 32), (1, 16))),
        "ocean_mask": draw_ocean_mask(jax.random.fold_in(keys[11], 71), 0),
        "band_plan": draw_band_plan(jax.random.fold_in(keys[11], 71), 0),
        "up_weight": scatter_about(keys[3], (3, 3, C, C), C ** -0.5, 0.75),
        "up_bias": scatter_about(keys[4], (C,), 0.5, 3.0, (), jnp.float32),
        "first_weight": scatter_about(keys[5], (3, 3, C, C), (9 * C) ** -0.5, 0.25),
        "first_bias": scatter_about(keys[6], (C,), 0.5, 3.0, (), jnp.float32),
        "second_weight": scatter_about(keys[7], (3, 3, C, C), (9 * C) ** -0.5, 0.25),
        "second_bias": scatter_about(keys[8], (C,), 0.5, 3.0, (), jnp.float32),
        "head_weight": scatter_about(keys[9], (C, FIELDS), C ** -0.5, 0.75),
        "head_bias": scatter_about(keys[10], (FIELDS,), 0.5, 3.0, (), jnp.float32),
    }


def gelu_tanh(values):
    return jax.nn.gelu(values, approximate=True)


def conv_valid(merged, weight):
    channels = weight.shape[2]
    height = merged.shape[0] - 2
    breadth = merged.shape[1] // channels - 2
    summed = jnp.zeros((height * breadth, channels), jnp.float32)
    for row_tap in range(3):
        for col_tap in range(3):
            window = merged[row_tap:row_tap + height, col_tap * channels:(col_tap + breadth) * channels]
            summed = summed + jnp.dot(window.reshape(height * breadth, channels), weight[row_tap, col_tap], preferred_element_type=jnp.float32)
    return summed.reshape(height, breadth, channels)


def expand_block(patch_in, row_masks, up_weight, up_bias, first_weight, first_bias, second_weight, second_bias, head_weight, head_bias):
    channels = up_weight.shape[2]
    fields_count = head_weight.shape[1]
    block_rows = patch_in.shape[0] - 2
    block_cols = patch_in.shape[1] // channels - 2
    up_matrix = up_weight.transpose(2, 0, 1, 3).reshape(channels, 9 * channels)
    lifted = jnp.dot(patch_in.reshape((block_rows + 2) * (block_cols + 2), channels), up_matrix, preferred_element_type=jnp.float32)
    lifted = lifted.reshape(block_rows + 2, block_cols + 2, 3, 3, channels) + up_bias
    lifted = lifted.transpose(0, 2, 1, 3, 4).reshape(3 * block_rows + 6, 3 * block_cols + 6, channels)
    fine_mask = jnp.repeat(row_masks, 3)[:, None, None]
    layer_zero = (gelu_tanh(lifted) * fine_mask).astype(jnp.bfloat16)
    layer_zero = layer_zero[1:-1, 1:-1].reshape(3 * block_rows + 4, (3 * block_cols + 4) * channels)
    second = gelu_tanh(conv_valid(layer_zero, first_weight) + first_bias) * fine_mask[2:-2]
    second = second.astype(jnp.bfloat16)
    skip_path = second[1:-1, 1:-1].astype(jnp.float32)
    second = second.reshape(3 * block_rows + 2, (3 * block_cols + 2) * channels)
    layer_two = (skip_path + gelu_tanh(conv_valid(second, second_weight) + second_bias)) * fine_mask[3:-3]
    layer_two = layer_two.astype(jnp.bfloat16)
    result = jnp.dot(layer_two.reshape(9 * block_rows * block_cols, channels), head_weight, preferred_element_type=jnp.float32) + head_bias
    return result.reshape(block_rows, 3, 3 * block_cols * fields_count)


def reference(coarse, ocean_mask, band_plan, up_weight, up_bias, first_weight, first_bias, second_weight, second_bias, head_weight, head_bias):
    channels = up_weight.shape[2]
    wrapped = jnp.concatenate([coarse[:, -channels:], coarse, coarse[:, :channels]], axis=1)
    border = jnp.zeros((1, wrapped.shape[1]), jnp.bfloat16)
    padded = jnp.concatenate([border, wrapped, border], axis=0)
    ocean_float = jnp.concatenate([jnp.zeros((1,), jnp.float32), ocean_mask.astype(jnp.float32), jnp.zeros((1,), jnp.float32)])
    row_ids = jnp.arange(LAT_IN, dtype=jnp.int32)
    sort_keys = jnp.where(ocean_mask == 1, band_plan * LAT_IN + row_ids, N_LAT * LAT_IN + row_ids)
    chosen = jnp.argsort(sort_keys, stable=True)[:SLOTS].astype(jnp.int32)

    def one_slot(slot_row):
        patch_rows = lax.dynamic_slice_in_dim(padded, slot_row, 3, 0)
        flag_rows = lax.dynamic_slice_in_dim(ocean_float, slot_row, 3, 0)
        return expand_block(patch_rows, flag_rows, up_weight, up_bias, first_weight, first_bias, second_weight, second_bias, head_weight, head_bias)[0]

    return lax.map(one_slot, chosen)
```

```python
from functools import partial

import jax
import jax.numpy as jnp
import numpy as np
from jax import lax
from jax.experimental import pallas as pl
from jax.experimental.pallas import tpu as pltpu
from jax.sharding import PartitionSpec as P

MESH = pl.DeviceIdType.MESH
BF = jnp.bfloat16
F32 = jnp.float32
ROWS = 64
SUB = 16
TILES = ROWS // SUB
LANES = 128
PAIRS = 32
GROUP = 11
CHUNKS = 3
SPAN = 32
SLOPE = float(np.sqrt(2.0 / np.pi))


def dot(a, b):
    return jnp.dot(a, b, preferred_element_type=F32)


def dot_t(a, b):
    return lax.dot_general(a, b, (((1,), (1,)), ((), ())), preferred_element_type=F32)


def iota(shape, dim):
    return lax.broadcasted_iota(jnp.int32, shape, dim)


def gelu_of_half(h):
    return h + h * jnp.tanh(h * (2 * SLOPE + (8 * 0.044715 * SLOPE) * (h * h)))


def place_of(m):
    return (m % SUB) * TILES + m // SUB


def store_layer(ref, at, a, value, masks):
    rounded = value.astype(BF)
    ref[at, a + 1] = rounded
    if a == 2:
        rolled = pltpu.roll(value[ROWS - SUB :], 1, 0).astype(BF)
        ref[at, 0, 0:SUB] = rolled * masks[0, 0:SUB]
        for t in range(1, TILES):
            low = t * SUB
            ref[at, 0, low : low + SUB] = rounded[low - SUB : low] * masks[0, low : low + SUB]
    if a == 0:
        for t in range(TILES - 1):
            low = t * SUB
            ref[at, 4, low : low + SUB] = (
                rounded[low + SUB : low + 2 * SUB] * masks[1, low : low + SUB]
            )
        rolled = pltpu.roll(value[:SUB], SUB - 1, 0).astype(BF)
        ref[at, 4, ROWS - SUB :] = rolled * masks[1, ROWS - SUB :]


def widen(weight_ref):
    channels = weight_ref.shape[-1]
    taps = weight_ref[...].reshape(-1, channels)
    row, lane = iota((channels, LANES), 0), iota((channels, LANES), 1)
    halves = []
    for shift in (0, channels):
        wide = dot(taps, (lane == row + shift).astype(BF)) * 0.5
        wide = wide.astype(BF)
        halves.append(
            [
                [wide[(p * 3 + q) * channels : (p * 3 + q + 1) * channels] for q in range(3)]
                for p in range(3)
            ]
        )
    return halves


def build_conv(weight_ref, w_pair, w_one, layer):
    low, high = widen(weight_ref)
    zero = jnp.zeros((256, LANES), BF)
    blocks = [
        jnp.concatenate(
            [low[p][0], low[p][1] + high[p][0], low[p][2] + high[p][1], high[p][2]], axis=0
        )
        for p in range(3)
    ]
    for i in range(4):
        at = slice(i * 256, (i + 1) * 256)
        w_pair[layer, at, 0:LANES] = blocks[i] if i < 3 else zero
        w_pair[layer, at, LANES:] = blocks[i - 1] if i > 0 else zero
    for i in range(3):
        w_one[layer, i * 256 : (i + 1) * 256, :] = blocks[i]


def build_up(weight_ref, w_up):
    low, high = widen(weight_ref)
    zero = jnp.zeros((64, LANES), BF)
    for a in range(3):
        first = [low[a][0] + high[a][1], low[a][2], zero]
        second = [zero, high[a][0], low[a][1] + high[a][2]]
        for n in range(3):
            at = slice(n * LANES, (n + 1) * LANES)
            w_up[a, 0:64, at] = first[n]
            w_up[a, 64:128, at] = second[n]


def build_head(weight_ref, w_head):
    fields = weight_ref.shape[1]
    row, lane = iota((fields, LANES), 0), iota((fields, LANES), 1)
    tiled = dot(weight_ref[...], (lane % fields == row).astype(BF))
    pixel = iota(tiled.shape, 1) // fields
    for p in range(16):
        for part, v in enumerate((0, 1, 1, 0)):
            block = jnp.where(pixel == 2 * p + v, tiled, 0.0).astype(BF)
            w_head[p, part * 64 : (part + 1) * 64, :] = block


def conv(ref, w_pair, w_one, bias, layer, at, count):
    pieces = [
        [ref[pl.ds(at + d, count), i].reshape(count * ROWS, LANES) for d in range(2)]
        for i in range(5)
    ]
    both = dot(jnp.concatenate(sum(pieces[:4], []), axis=1), w_pair[layer])
    last = dot(jnp.concatenate(sum(pieces[2:], []), axis=1), w_one[layer])
    rows = [both[:, :LANES], both[:, LANES:], last]
    return [gelu_of_half(z + bias) for z in rows]


def kernel(
    lat_count,
    lon_count,
    x_ref,
    ocean_ref,
    band_ref,
    up_weight,
    up_bias,
    first_weight,
    first_bias,
    second_weight,
    second_bias,
    head_weight,
    head_bias,
    out_ref,
    edge,
    halo,
    corner,
    side,
    xc,
    zero_layer,
    one_layer,
    grown,
    w_up,
    w_pair,
    w_one,
    w_head,
    masks,
    spread,
    gather,
    outgoing,
    incoming,
    halo_send,
    halo_recv,
    out_send,
    out_recv,
):
    me = lax.axis_index("lat")
    lon = lax.axis_index("lon")
    north, south = (me + lat_count - 1) % lat_count, (me + 1) % lat_count
    west, east = (lon + lon_count - 1) % lon_count, (lon + 1) % lon_count
    width = x_ref.shape[1]

    barrier = pltpu.get_barrier_semaphore()

    def greet(t, carry):
        pl.semaphore_signal(
            barrier,
            inc=1,
            device_id={"lat": (me + t) % lat_count, "lon": lon},
            device_id_type=MESH,
        )
        return carry

    lax.fori_loop(1, lat_count, greet, 0)
    others = [(me, west), (me, east)] + [(r, c) for r in (north, south) for c in (west, east)]
    for r, c in others:
        pl.semaphore_signal(
            barrier, inc=1, device_id={"lat": r, "lon": c}, device_id_type=MESH
        )

    edge[0] = x_ref[0:SUB, :].astype(F32)[0:1]
    edge[1] = x_ref[ROWS - SUB :, :].astype(F32)[SUB - 1 :]

    pl.semaphore_wait(barrier, lat_count - 1 + len(others))
    first, final = pl.ds(0, LANES), pl.ds(width - LANES, LANES)
    plan = [
        (edge.at[0], halo.at[1], north, lon),
        (edge.at[1], halo.at[0], south, lon),
        (x_ref.at[:, first], side.at[0], me, west),
        (x_ref.at[:, final], side.at[1], me, east),
        (edge.at[0, :, first], corner.at[1, 0], north, west),
        (edge.at[0, :, final], corner.at[1, 1], north, east),
        (edge.at[1, :, first], corner.at[0, 0], south, west),
        (edge.at[1, :, final], corner.at[0, 1], south, east),
    ]
    copies = []
    for n, (source, target, r, c) in enumerate(plan):
        copy = pltpu.make_async_remote_copy(
            src_ref=source,
            dst_ref=target,
            send_sem=halo_send.at[n],
            recv_sem=halo_recv.at[n],
            device_id={"lat": r, "lon": c},
            device_id_type=MESH,
        )
        copy.start()
        copies.append(copy)

    row, col = iota((ROWS, ROWS), 0), iota((ROWS, ROWS), 1)
    source = iota((LANES, ROWS), 0) == (me % 2) * ROWS + iota((LANES, ROWS), 1)
    source = source.astype(BF)
    ocean_all = ocean_ref[...].astype(F32).astype(BF)
    band_all = band_ref[...].astype(F32).astype(BF)
    half_rows = ocean_all.shape[0]
    mine = (iota((SUB, half_rows), 1) == me // 2).astype(BF)
    ocean_row = dot(dot(mine, ocean_all).astype(BF), source)[0:1]
    band_row = dot(dot(mine, band_all).astype(BF), source)[0:1]
    eye = (row == col).astype(F32)
    before = (row < col).astype(F32)
    ocean_col = jnp.sum(eye * ocean_row, axis=1, keepdims=True)
    band_col = jnp.sum(eye * band_row, axis=1, keepdims=True)
    order_row = jnp.sum(before * ocean_col, axis=0, keepdims=True) + 1.0
    order_col = jnp.sum((col < row).astype(F32) * ocean_row, axis=1, keepdims=True) + 1.0
    total = jnp.sum(ocean_row, axis=1, keepdims=True)
    place = place_of(row).astype(F32)
    pick = jnp.where(place == order_row, ocean_row, 0.0)
    top = (place[:, 0:1] == 0.0).astype(F32)
    bottom = (place[:, 0:1] == total + 1.0).astype(F32)
    has_north = jnp.where(me > 0, 1.0, 0.0)
    has_south = jnp.where(me < lat_count - 1, 1.0, 0.0)
    above = jnp.sum((row + 1 == col).astype(F32) * ocean_col, axis=0, keepdims=True)
    above = above + jnp.where(col[0:1] == 0, has_north, 0.0)
    below = jnp.sum((row == col + 1).astype(F32) * ocean_col, axis=0, keepdims=True)
    below = below + jnp.where(col[0:1] == ROWS - 1, has_south, 0.0)
    up_mask = jnp.sum(pick * above, axis=1, keepdims=True) + bottom
    down_mask = jnp.sum(pick * below, axis=1, keepdims=True) + top
    masks[0] = jnp.broadcast_to(up_mask, (ROWS, LANES)).astype(BF)
    masks[1] = jnp.broadcast_to(down_mask, (ROWS, LANES)).astype(BF)

    earlier = jnp.where(band_col == band_row, before, 0.0) * ocean_col
    turn_row = jnp.sum(earlier, axis=0, keepdims=True)
    line = iota((lat_count * SUB, ROWS), 0)
    slot = (line // SUB * 2 + line % SUB // 6).astype(F32)
    fits = (slot == band_row * 2.0 + turn_row) & (line % SUB < 12)
    leaves = jnp.where(fits, ocean_row, 0.0).astype(BF)
    lane = iota((ROWS, 6 * ROWS), 1)
    there = place_of(lane % ROWS).astype(F32) == order_col
    there = jnp.where(there, ocean_col, 0.0).astype(BF)
    moved = dot(leaves, there)
    line, lane = iota(moved.shape, 0), iota(moved.shape, 1)
    spread[...] = jnp.where(line % SUB % 6 == lane // ROWS, moved, 0.0).astype(BF)

    arrive = jnp.where(band_all.astype(F32) == me.astype(F32), ocean_all.astype(F32), 0.0)
    width_in = lat_count * SUB
    home = iota((LANES, width_in), 1) // SUB
    counts = dot(arrive.astype(BF), (iota((LANES, width_in), 0) // ROWS == home % 2).astype(BF))
    home = iota(counts.shape, 1) // SUB
    count_row = jnp.sum(
        jnp.where(iota(counts.shape, 0) == home // 2, counts, 0.0), axis=0, keepdims=True
    )
    sooner = jnp.where(iota(counts.shape, 0) < home // 2, counts, 0.0)
    other = dot(arrive.astype(BF), (iota((LANES, width_in), 0) // ROWS != iota((LANES, width_in), 1) // SUB % 2).astype(BF))
    sooner = sooner + jnp.where(iota(counts.shape, 0) < home // 2, other, 0.0)
    sooner = sooner + jnp.where(
        (iota(counts.shape, 0) == home // 2) & (home % 2 == 1), other, 0.0
    )
    base_row = jnp.sum(sooner, axis=0, keepdims=True)
    slots = out_ref.shape[0]
    shape = (2 * slots * 4, width_in)
    line, lane = iota(shape, 0), iota(shape, 1)
    turn = lane % SUB // 6
    part = lane % SUB % 6
    wanted = (line // (slots * 4)) * 3 + line % 4
    number = (line // 4 % slots - turn).astype(F32)
    hit = (number == base_row) & (turn.astype(F32) < count_row)
    hit = hit & (part == wanted) & (line % 4 < 3) & (lane % SUB < 12)
    gather[...] = jnp.where(hit, 1.0, 0.0).astype(BF)

    build_up(up_weight, w_up)
    build_conv(first_weight, w_pair, w_one, 0)
    build_conv(second_weight, w_pair, w_one, 1)
    build_head(head_weight, w_head)
    bias_up, bias_one, bias_two = (
        jnp.concatenate([b[...], b[...]], axis=1) * 0.5 for b in (up_bias, first_bias, second_bias)
    )
    bias_head = jnp.concatenate([head_bias[...]] * (LANES // head_bias.shape[1]), axis=1)

    for copy in copies:
        copy.wait()

    ends = iota((ROWS, SUB), 1)
    pick_ends = jnp.where(ends == 0, top, jnp.where(ends == 1, bottom, 0.0))
    pick_all = jnp.concatenate([pick.astype(BF), pick_ends.astype(BF)], axis=1)

    def two_rows(upper, lower):
        which = iota((SUB, upper.shape[1]), 0)
        return jnp.where(which == 0, upper, jnp.where(which == 1, lower, 0.0)).astype(BF)

    lifted = dot(
        pick_all, jnp.concatenate([x_ref[...], two_rows(halo[0], halo[1])], axis=0)
    ).astype(BF)
    for j in range(PAIRS):
        xc[j] = lifted[:, j * LANES : (j + 1) * LANES]
    low_lanes = iota((1, LANES), 1) < 64
    joined = jnp.where(low_lanes, side[0].astype(F32), side[1].astype(F32)).astype(BF)
    joined_ends = two_rows(
        jnp.where(low_lanes, corner[0, 0], corner[0, 1]),
        jnp.where(low_lanes, corner[1, 0], corner[1, 1]),
    )
    outer = dot(pick_all, jnp.concatenate([joined, joined_ends], axis=0)).astype(BF)
    for a in range(3):
        z = dot(outer, w_up[a])
        for n, at in ((2, 0), (0, 3 * PAIRS + 1)):
            grow = gelu_of_half(z[:, n * LANES : (n + 1) * LANES] + bias_up)
            store_layer(zero_layer, at, a, grow, masks)

    def chunk(c, carry):
        start = jnp.minimum(c * GROUP, PAIRS - GROUP)
        source = xc[pl.ds(start, GROUP)].reshape(GROUP * ROWS, LANES)
        for a in range(3):
            z = dot(source, w_up[a])
            for n in range(3):
                grow = gelu_of_half(z[:, n * LANES : (n + 1) * LANES] + bias_up)
                for j in range(GROUP):
                    value = grow[j * ROWS : (j + 1) * ROWS]
                    store_layer(zero_layer, 3 * (start + j) + 1 + n, a, value, masks)

        base = c * SPAN
        step = 11

        def first(g, carry):
            at = base + g * step
            rows = conv(zero_layer, w_pair, w_one, bias_one, 0, at, step)
            for a in range(3):
                for j in range(step):
                    store_layer(one_layer, at + j, a, rows[a][j * ROWS : (j + 1) * ROWS], masks)
            return carry

        lax.fori_loop(0, (SPAN + 1) // step, first, 0)
        stride = 8

        def second(g, carry):
            rows = conv(one_layer, w_pair, w_one, bias_two, 1, base + g * stride, stride)
            for a in range(3):
                grown[pl.ds(g * stride, stride), a] = (
                    rows[a].astype(BF).reshape(stride, ROWS, LANES)
                )
            return carry

        lax.fori_loop(0, SPAN // stride, second, 0)

        pieces = []
        high = jnp.where(low_lanes, 0.0, 1.0).astype(BF)
        low = jnp.where(low_lanes, 1.0, 0.0).astype(BF)
        for p in range(16):
            skip = [
                one_layer[base + t * 16 + p + 1, 1:4] * low
                + one_layer[base + t * 16 + p, 1:4] * high
                for t in range(2)
            ]
            made = [grown[t * 16 + p] for t in range(2)]
            for part in (made, skip):
                pieces.append(jnp.concatenate([v.reshape(3 * ROWS, LANES) for v in part], axis=0))
        fields = dot(jnp.concatenate(pieces, axis=1), w_head[...].reshape(16 * 256, LANES))
        fields = (fields + bias_head).astype(BF)
        outgoing[c] = dot(spread[...], fields).astype(BF).reshape(lat_count, SUB, LANES)

        def send(t, carry):
            target = (me + t) % lat_count
            pltpu.make_async_remote_copy(
                src_ref=outgoing.at[c, target],
                dst_ref=incoming.at[c, me],
                send_sem=out_send.at[c],
                recv_sem=out_recv.at[c],
                device_id={"lat": target, "lon": lon},
                device_id_type=MESH,
            ).start()
            return carry

        lax.fori_loop(1, lat_count, send, 0)
        incoming[c, me] = outgoing[c, me]
        return carry

    lax.fori_loop(0, CHUNKS, chunk, 0)

    for c in range(CHUNKS):
        rest = pl.ds(0, lat_count - 1)
        pltpu.make_async_copy(incoming.at[c, rest], incoming.at[c, rest], out_recv.at[c]).wait()
        landed = incoming[c].reshape(lat_count * SUB, LANES)
        made = dot(gather[...], landed)
        for t in range(2):
            block = made[t * slots * 4 : (t + 1) * slots * 4].reshape(slots, 4, LANES)
            at = (2 * c + t) * LANES
            out_ref[:, :, at : at + LANES] = block[:, 0:3]
    for c in range(CHUNKS):
        rest = pl.ds(0, lat_count - 1)
        pltpu.make_async_copy(outgoing.at[c, rest], outgoing.at[c, rest], out_send.at[c]).wait()


def body(lat_count, lon_count, coarse, ocean_mask, band_plan, up_weight, up_bias, first_weight,
         first_bias, second_weight, second_bias, head_weight, head_bias):
    slots = 32
    vmem = pl.BlockSpec(memory_space=pltpu.VMEM)
    row = lambda v: v.reshape(1, -1)
    return pl.pallas_call(
        partial(kernel, lat_count, lon_count),
        out_shape=jax.ShapeDtypeStruct((slots, 3, 768), F32),
        in_specs=[vmem] * 11,
        out_specs=vmem,
        scratch_shapes=[
            pltpu.VMEM((2, 1, coarse.shape[1]), F32),
            pltpu.VMEM((2, 1, coarse.shape[1]), F32),
            pltpu.VMEM((2, 2, 1, LANES), F32),
            pltpu.VMEM((2, ROWS, LANES), BF),
            pltpu.VMEM((PAIRS, ROWS, LANES), BF),
            pltpu.VMEM((3 * PAIRS + 2, 5, ROWS, LANES), BF),
            pltpu.VMEM((3 * PAIRS + 1, 5, ROWS, LANES), BF),
            pltpu.VMEM((SPAN, 3, ROWS, LANES), BF),
            pltpu.VMEM((3, LANES, 3 * LANES), BF),
            pltpu.VMEM((2, 1024, 2 * LANES), BF),
            pltpu.VMEM((2, 768, LANES), BF),
            pltpu.VMEM((16, 256, LANES), BF),
            pltpu.VMEM((2, ROWS, LANES), BF),
            pltpu.VMEM((lat_count * SUB, 6 * ROWS), BF),
            pltpu.VMEM((2 * slots * 4, lat_count * SUB), BF),
            pltpu.VMEM((CHUNKS, lat_count, SUB, LANES), BF),
            pltpu.VMEM((CHUNKS, lat_count, SUB, LANES), BF),
            pltpu.SemaphoreType.DMA((8,)),
            pltpu.SemaphoreType.DMA((8,)),
            pltpu.SemaphoreType.DMA((CHUNKS,)),
            pltpu.SemaphoreType.DMA((CHUNKS,)),
        ],
        compiler_params=pltpu.CompilerParams(
            collective_id=0, has_side_effects=True, vmem_limit_bytes=60 * 2**20
        ),
    )(
        coarse,
        ocean_mask.reshape(-1, LANES),
        band_plan.reshape(-1, LANES),
        up_weight,
        row(up_bias),
        first_weight,
        row(first_bias),
        second_weight,
        row(second_bias),
        head_weight,
        row(head_bias),
    )


def solution(mesh):
    in_specs = (P("lat", "lon"), P(), P(), P(), P(), P(), P(), P(), P(), P(), P())
    out_specs = P("lat", None, "lon")
    call = partial(body, mesh.shape["lat"], mesh.shape["lon"])
    return jax.shard_map(call, mesh=mesh, in_specs=in_specs, out_specs=out_specs, check_vma=False)
```

```python
from functools import partial

import jax
import jax.numpy as jnp
import numpy as np
from jax import lax
from jax.experimental import pallas as pl
from jax.experimental.pallas import tpu as pltpu
from jax.sharding import PartitionSpec as P

MESH = pl.DeviceIdType.MESH
BF = jnp.bfloat16
F32 = jnp.float32
ROWS = 64
SENT = 12
SUB = 16
TILES = ROWS // SUB
LANES = 128
PAIRS = 32
CHUNKS = 3
SPAN = 32
SLOPE = float(np.sqrt(2.0 / np.pi))


def dot(a, b):
    return jnp.dot(a, b, preferred_element_type=F32)


def dot_t(a, b):
    return lax.dot_general(a, b, (((1,), (1,)), ((), ())), preferred_element_type=F32)


def iota(shape, dim):
    return lax.broadcasted_iota(jnp.int32, shape, dim)


def gelu_of_half(h):
    h = h.astype(BF)
    return h + h * jnp.tanh(h * (BF(2 * SLOPE) + BF(8 * 0.044715 * SLOPE) * (h * h)))


def place_of(m):
    return (m % SUB) * TILES + m // SUB


def store_layer(ref, at, a, value, masks):
    rounded = value
    ref[at, a + 1] = rounded
    if a == 2:
        rolled = pltpu.roll(value[ROWS - SUB :].astype(F32), 1, 0).astype(BF)
        ref[at, 0, 0:SUB] = rolled * masks[0, 0:SUB]
        for t in range(1, TILES):
            low = t * SUB
            ref[at, 0, low : low + SUB] = rounded[low - SUB : low] * masks[0, low : low + SUB]
    if a == 0:
        for t in range(TILES - 1):
            low = t * SUB
            ref[at, 4, low : low + SUB] = (
                rounded[low + SUB : low + 2 * SUB] * masks[1, low : low + SUB]
            )
        rolled = pltpu.roll(value[:SUB].astype(F32), SUB - 1, 0).astype(BF)
        ref[at, 4, ROWS - SUB :] = rolled * masks[1, ROWS - SUB :]


def widen(weight_ref):
    channels = weight_ref.shape[-1]
    taps = weight_ref[...].reshape(-1, channels)
    row, lane = iota((channels, LANES), 0), iota((channels, LANES), 1)
    halves = []
    for shift in (0, channels):
        wide = dot(taps, (lane == row + shift).astype(BF)) * 0.5
        wide = wide.astype(BF)
        halves.append(
            [
                [wide[(p * 3 + q) * channels : (p * 3 + q + 1) * channels] for q in range(3)]
                for p in range(3)
            ]
        )
    return halves


def build_conv(weight_ref, w_pair, w_one, layer):
    low, high = widen(weight_ref)
    if layer == 1:
        low, high = high, low
    zero = jnp.zeros((256, LANES), BF)
    blocks = [
        jnp.concatenate(
            [low[p][0], low[p][1] + high[p][0], low[p][2] + high[p][1], high[p][2]], axis=0
        )
        for p in range(3)
    ]
    for i in range(4):
        at = slice(i * 256, (i + 1) * 256)
        w_pair[layer, at, 0:LANES] = blocks[i] if i < 3 else zero
        w_pair[layer, at, LANES:] = blocks[i - 1] if i > 0 else zero
    for i in range(3):
        w_one[layer, i * 256 : (i + 1) * 256, :] = blocks[i]


def build_up(weight_ref, w_up):
    low, high = widen(weight_ref)
    zero = jnp.zeros((64, LANES), BF)
    for a in range(3):
        first = [low[a][0] + high[a][1], low[a][2], zero]
        second = [zero, high[a][0], low[a][1] + high[a][2]]
        for n in range(3):
            at = slice((3 * a + n) * LANES, (3 * a + n + 1) * LANES)
            w_up[0:64, at] = first[n]
            w_up[64:128, at] = second[n]


def build_head(weight_ref, w_head):
    fields = weight_ref.shape[0]
    row, lane = iota((fields, LANES), 0), iota((fields, LANES), 1)
    tiled = lax.dot_general(
        weight_ref[...],
        (lane % fields == row).astype(BF),
        (((0,), (0,)), ((), ())),
        preferred_element_type=F32,
    )
    pixel = iota(tiled.shape, 1) // fields
    for p in range(16):
        for part, v in enumerate((1, 0)):
            block = jnp.where(pixel == 2 * p + v, tiled, 0.0).astype(BF)
            at = p * LANES + part * 64
            w_head[at : at + 64, :] = block


def conv(ref, w_pair, w_one, bias, layer, at, count):
    pieces = [
        [ref[pl.ds(at + d, count), i].reshape(count * ROWS, LANES) for d in range(2)]
        for i in range(5)
    ]
    both = dot(jnp.concatenate(sum(pieces[:4], []), axis=1), w_pair[layer])
    last = dot(jnp.concatenate(sum(pieces[2:], []), axis=1), w_one[layer])
    rows = [both[:, :LANES], both[:, LANES:], last]
    return [gelu_of_half(z + bias) for z in rows]


def kernel(
    lat_count,
    lon_count,
    x_ref,
    ocean_ref,
    band_ref,
    up_weight,
    up_bias,
    first_weight,
    first_bias,
    second_weight,
    second_bias,
    head_weight,
    head_bias,
    out_ref,
    edge,
    halo,
    corner,
    side,
    xc,
    zero_layer,
    one_layer,
    grown,
    w_up,
    w_pair,
    w_one,
    w_head,
    masks,
    spread,
    gather,
    outgoing,
    incoming,
    halo_send,
    halo_recv,
    out_send,
    out_recv,
):
    me = lax.axis_index("lat")
    lon = lax.axis_index("lon")
    north, south = (me + lat_count - 1) % lat_count, (me + 1) % lat_count
    west, east = (lon + lon_count - 1) % lon_count, (lon + 1) % lon_count
    width = x_ref.shape[1]

    barrier = pltpu.get_barrier_semaphore()

    def greet(t, carry):
        pl.semaphore_signal(
            barrier,
            inc=1,
            device_id={"lat": (me + t) % lat_count, "lon": lon},
            device_id_type=MESH,
        )
        return carry

    lax.fori_loop(1, lat_count, greet, 0)
    others = [(me, west), (me, east)] + [(r, c) for r in (north, south) for c in (west, east)]
    for r, c in others:
        pl.semaphore_signal(
            barrier, inc=1, device_id={"lat": r, "lon": c}, device_id_type=MESH
        )

    build_up(up_weight, w_up)
    build_conv(first_weight, w_pair, w_one, 0)
    build_conv(second_weight, w_pair, w_one, 1)
    build_head(head_weight, w_head)

    edge[0] = x_ref[0:SUB, :].astype(F32)[0:1]
    edge[1] = x_ref[ROWS - SUB :, :].astype(F32)[SUB - 1 :]

    pl.semaphore_wait(barrier, lat_count - 1 + len(others))
    first, final = pl.ds(0, LANES), pl.ds(width - LANES, LANES)
    plan = [
        (edge.at[0], halo.at[1], north, lon),
        (edge.at[1], halo.at[0], south, lon),
        (x_ref.at[:, first], side.at[0], me, west),
        (x_ref.at[:, final], side.at[1], me, east),
        (edge.at[0, :, first], corner.at[1, 0], north, west),
        (edge.at[0, :, final], corner.at[1, 1], north, east),
        (edge.at[1, :, first], corner.at[0, 0], south, west),
        (edge.at[1, :, final], corner.at[0, 1], south, east),
    ]
    copies = []
    for n, (source, target, r, c) in enumerate(plan):
        copy = pltpu.make_async_remote_copy(
            src_ref=source,
            dst_ref=target,
            send_sem=halo_send.at[n],
            recv_sem=halo_recv.at[n],
            device_id={"lat": r, "lon": c},
            device_id_type=MESH,
        )
        copy.start()
        copies.append(copy)

    row, col = iota((ROWS, ROWS), 0), iota((ROWS, ROWS), 1)
    source = iota((LANES, ROWS), 0) == (me % 2) * ROWS + iota((LANES, ROWS), 1)
    source = source.astype(BF)
    ocean_all = ocean_ref[...].astype(F32).astype(BF)
    band_all = band_ref[...].astype(F32).astype(BF)
    half_rows = ocean_all.shape[0]
    mine = (iota((SUB, half_rows), 1) == me // 2).astype(BF)
    ocean_row = dot(dot(mine, ocean_all).astype(BF), source)[0:1]
    band_row = dot(dot(mine, band_all).astype(BF), source)[0:1]
    eye = (row == col).astype(F32)
    before = (row < col).astype(F32)
    ocean_col = jnp.sum(eye * ocean_row, axis=1, keepdims=True)
    band_col = jnp.sum(eye * band_row, axis=1, keepdims=True)
    order_row = jnp.sum(before * ocean_col, axis=0, keepdims=True) + 1.0
    order_col = jnp.sum((col < row).astype(F32) * ocean_row, axis=1, keepdims=True) + 1.0
    total = jnp.sum(ocean_row, axis=1, keepdims=True)
    place = place_of(row).astype(F32)
    pick = jnp.where(place == order_row, ocean_row, 0.0)
    top = (place[:, 0:1] == 0.0).astype(F32)
    bottom = (place[:, 0:1] == total + 1.0).astype(F32)
    has_north = jnp.where(me > 0, 1.0, 0.0)
    has_south = jnp.where(me < lat_count - 1, 1.0, 0.0)
    above = jnp.sum((row + 1 == col).astype(F32) * ocean_col, axis=0, keepdims=True)
    above = above + jnp.where(col[0:1] == 0, has_north, 0.0)
    below = jnp.sum((row == col + 1).astype(F32) * ocean_col, axis=0, keepdims=True)
    below = below + jnp.where(col[0:1] == ROWS - 1, has_south, 0.0)
    up_mask = jnp.sum(pick * above, axis=1, keepdims=True) + bottom
    down_mask = jnp.sum(pick * below, axis=1, keepdims=True) + top
    masks[0] = jnp.broadcast_to(up_mask, (ROWS, LANES)).astype(BF)
    masks[1] = jnp.broadcast_to(down_mask, (ROWS, LANES)).astype(BF)

    earlier = jnp.where(band_col == band_row, before, 0.0) * ocean_col
    turn_row = jnp.sum(earlier, axis=0, keepdims=True)
    line = iota((lat_count * SENT, ROWS), 0)
    slot = (line // SENT * 2 + line % SENT // 6).astype(F32)
    leaves = jnp.where(slot == band_row * 2.0 + turn_row, ocean_row, 0.0).astype(BF)
    lane = iota((ROWS, 6 * ROWS), 1)
    there = place_of(lane % ROWS).astype(F32) == order_col
    there = jnp.where(there, ocean_col, 0.0).astype(BF)
    moved = dot(leaves, there)
    line, lane = iota(moved.shape, 0), iota(moved.shape, 1)
    spread[...] = jnp.where(line % 6 == lane // ROWS, moved, 0.0).astype(BF)

    arrive = jnp.where(band_all.astype(F32) == me.astype(F32), ocean_all.astype(F32), 0.0)
    width_in = lat_count * SENT
    home = iota((LANES, width_in), 1) // SENT
    counts = dot(arrive.astype(BF), (iota((LANES, width_in), 0) // ROWS == home % 2).astype(BF))
    home = iota(counts.shape, 1) // SENT
    count_row = jnp.sum(
        jnp.where(iota(counts.shape, 0) == home // 2, counts, 0.0), axis=0, keepdims=True
    )
    sooner = jnp.where(iota(counts.shape, 0) < home // 2, counts, 0.0)
    other = dot(arrive.astype(BF), (iota((LANES, width_in), 0) // ROWS != iota((LANES, width_in), 1) // SENT % 2).astype(BF))
    sooner = sooner + jnp.where(iota(counts.shape, 0) < home // 2, other, 0.0)
    sooner = sooner + jnp.where(
        (iota(counts.shape, 0) == home // 2) & (home % 2 == 1), other, 0.0
    )
    base_row = jnp.sum(sooner, axis=0, keepdims=True)
    slots = out_ref.shape[1]
    shape = (6 * slots, width_in)
    line, lane = iota(shape, 0), iota(shape, 1)
    turn = lane % SENT // 6
    number = (line % slots - turn).astype(F32)
    hit = (number == base_row) & (turn.astype(F32) < count_row) & (lane % 6 == line // slots)
    gather[...] = jnp.where(hit, 1.0, 0.0).astype(BF)

    bias_up, bias_one, bias_two = (
        jnp.concatenate([b[...], b[...]], axis=1) * 0.5 for b in (up_bias, first_bias, second_bias)
    )
    bias_head = jnp.concatenate([head_bias[...]] * (LANES // head_bias.shape[1]), axis=1)

    for copy in copies[:2]:
        copy.wait()

    ends = iota((ROWS, SUB), 1)
    pick_ends = jnp.where(ends == 0, top, jnp.where(ends == 1, bottom, 0.0))
    pick_all = jnp.concatenate([pick.astype(BF), pick_ends.astype(BF)], axis=1)

    def two_rows(upper, lower):
        which = iota((SUB, upper.shape[1]), 0)
        return jnp.where(which == 0, upper, jnp.where(which == 1, lower, 0.0)).astype(BF)

    lifted = dot(
        pick_all, jnp.concatenate([x_ref[...], two_rows(halo[0], halo[1])], axis=0)
    ).astype(BF)
    for j in range(PAIRS):
        xc[j] = lifted[:, j * LANES : (j + 1) * LANES]
    low_lanes = iota((1, LANES), 1) < 64

    def outer_columns():
        for copy in copies[2:]:
            copy.wait()
        joined = jnp.where(low_lanes, side[0].astype(F32), side[1].astype(F32)).astype(BF)
        joined_ends = two_rows(
            jnp.where(low_lanes, corner[0, 0], corner[0, 1]),
            jnp.where(low_lanes, corner[1, 0], corner[1, 1]),
        )
        outer = dot(pick_all, jnp.concatenate([joined, joined_ends], axis=0)).astype(BF)
        z = dot(outer, w_up[...])
        for a in range(3):
            for n, at in ((2, 0), (0, 3 * PAIRS + 1)):
                grow = gelu_of_half(z[:, (3 * a + n) * LANES :][:, :LANES] + bias_up)
                store_layer(zero_layer, at, a, grow, masks)

    def chunk(c, start, group):
        source = xc[pl.ds(start, group)].reshape(group * ROWS, LANES)
        z = dot(source, w_up[...])
        for a in range(3):
            for n in range(3):
                grow = gelu_of_half(z[:, (3 * a + n) * LANES :][:, :LANES] + bias_up)
                for j in range(group):
                    value = grow[j * ROWS : (j + 1) * ROWS]
                    store_layer(zero_layer, 3 * (start + j) + 1 + n, a, value, masks)

        base = c * SPAN
        count = SPAN + 1
        rows = conv(zero_layer, w_pair, w_one, bias_one, 0, base, count)
        for a in range(3):
            for j in range(count):
                store_layer(one_layer, base + j, a, rows[a][j * ROWS : (j + 1) * ROWS], masks)

        rows = conv(one_layer, w_pair, w_one, bias_two, 1, base, SPAN)
        high = jnp.where(low_lanes, 0.0, 1.0).astype(BF)
        low = jnp.where(low_lanes, 1.0, 0.0).astype(BF)
        for a in range(3):
            for j in range(SPAN):
                skip = one_layer[base + j + 1, a + 1] * low + one_layer[base + j, a + 1] * high
                grown[j, a] = rows[a][j * ROWS : (j + 1) * ROWS] + skip

        pieces = []
        for p in range(16):
            made = [grown[t * 16 + p].reshape(3 * ROWS, LANES) for t in range(2)]
            pieces.append(jnp.concatenate(made, axis=0))
        fields = dot(jnp.concatenate(pieces, axis=1), w_head[...])
        fields = (fields + bias_head).astype(BF)
        outgoing[c] = dot(spread[...], fields).astype(BF).reshape(lat_count, SENT // 4, 4, LANES)

        def send(t, carry):
            target = (me + t) % lat_count
            pltpu.make_async_remote_copy(
                src_ref=outgoing.at[c, target],
                dst_ref=incoming.at[c, me],
                send_sem=out_send.at[c],
                recv_sem=out_recv.at[c],
                device_id={"lat": target, "lon": lon},
                device_id_type=MESH,
            ).start()
            return carry

        lax.fori_loop(1, lat_count, send, 0)
        incoming[c, me] = outgoing[c, me]

    chunk(1, 10, 12)
    outer_columns()
    chunk(2, 22, 10)
    chunk(0, 0, 10)

    for c in (1, 2, 0):
        rest = pl.ds(0, lat_count - 1)
        pltpu.make_async_copy(incoming.at[c, rest], incoming.at[c, rest], out_recv.at[c]).wait()
        landed = incoming[c].reshape(lat_count * SENT, LANES)
        made = dot(gather[...], landed)
        for t in range(2):
            for a in range(3):
                at = (t * 3 + a) * slots
                out_ref[a, :, pl.ds((2 * c + t) * LANES, LANES)] = made[at : at + slots]
    for c in (1, 2, 0):
        rest = pl.ds(0, lat_count - 1)
        pltpu.make_async_copy(outgoing.at[c, rest], outgoing.at[c, rest], out_send.at[c]).wait()


def body(lat_count, lon_count, coarse, ocean_mask, band_plan, up_weight, up_bias, first_weight,
         first_bias, second_weight, second_bias, head_weight, head_bias):
    slots = 32
    vmem = pl.BlockSpec(memory_space=pltpu.VMEM)
    row = lambda v: v.reshape(1, -1)
    made = pl.pallas_call(
        partial(kernel, lat_count, lon_count),
        out_shape=jax.ShapeDtypeStruct((3, slots, 768), F32),
        in_specs=[vmem] * 11,
        out_specs=vmem,
        scratch_shapes=[
            pltpu.VMEM((2, 1, coarse.shape[1]), F32),
            pltpu.VMEM((2, 1, coarse.shape[1]), F32),
            pltpu.VMEM((2, 2, 1, LANES), F32),
            pltpu.VMEM((2, ROWS, LANES), BF),
            pltpu.VMEM((PAIRS, ROWS, LANES), BF),
            pltpu.VMEM((3 * PAIRS + 2, 5, ROWS, LANES), BF),
            pltpu.VMEM((3 * PAIRS + 1, 5, ROWS, LANES), BF),
            pltpu.VMEM((SPAN, 3, ROWS, LANES), BF),
            pltpu.VMEM((LANES, 9 * LANES), BF),
            pltpu.VMEM((2, 1024, 2 * LANES), BF),
            pltpu.VMEM((2, 768, LANES), BF),
            pltpu.VMEM((16 * LANES, LANES), BF),
            pltpu.VMEM((2, ROWS, LANES), BF),
            pltpu.VMEM((lat_count * SENT, 6 * ROWS), BF),
            pltpu.VMEM((6 * slots, lat_count * SENT), BF),
            pltpu.VMEM((CHUNKS, lat_count, SENT // 4, 4, LANES), BF),
            pltpu.VMEM((CHUNKS, lat_count, SENT // 4, 4, LANES), BF),
            pltpu.SemaphoreType.DMA((8,)),
            pltpu.SemaphoreType.DMA((8,)),
            pltpu.SemaphoreType.DMA((CHUNKS,)),
            pltpu.SemaphoreType.DMA((CHUNKS,)),
        ],
        compiler_params=pltpu.CompilerParams(
            collective_id=0, has_side_effects=True, vmem_limit_bytes=60 * 2**20
        ),
    )(
        coarse,
        ocean_mask.reshape(-1, LANES),
        band_plan.reshape(-1, LANES),
        up_weight,
        row(up_bias),
        first_weight,
        row(first_bias),
        second_weight,
        row(second_bias),
        head_weight.T,
        row(head_bias),
    )
    return made.transpose(1, 0, 2)


def solution(mesh):
    in_specs = (P("lat", "lon"), P(), P(), P(), P(), P(), P(), P(), P(), P(), P())
    out_specs = P("lat", None, "lon")
    call = partial(body, mesh.shape["lat"], mesh.shape["lon"])
    return jax.shard_map(call, mesh=mesh, in_specs=in_specs, out_specs=out_specs, check_vma=False)
```

```python
from functools import partial

import jax
import jax.numpy as jnp
import numpy as np
from jax import lax
from jax.experimental import pallas as pl
from jax.experimental.pallas import tpu as pltpu
from jax.sharding import PartitionSpec as P

MESH = pl.DeviceIdType.MESH
BF = jnp.bfloat16
F32 = jnp.float32
ROWS = 64
SENT = 6
MOST = 2
WIDE = 16
SUB = 16
TILES = ROWS // SUB
LANES = 128
PAIRS = 32
PARTS = ((2, 3), (0, 2), (5, 1))
SLOPE = float(np.sqrt(2.0 / np.pi))


def dot(a, b):
    return jnp.dot(a, b, preferred_element_type=F32)


def dot_t(a, b):
    return lax.dot_general(a, b, (((1,), (1,)), ((), ())), preferred_element_type=F32)


def iota(shape, dim):
    return lax.broadcasted_iota(jnp.int32, shape, dim)


def gelu_of_half(h):
    h = h.astype(BF)
    return h + h * jnp.tanh(h * (BF(2 * SLOPE) + BF(8 * 0.044715 * SLOPE) * (h * h)))


def place_of(m):
    return (m % SUB) * TILES + m // SUB


def store_layer(ref, at, a, value, masks):
    rounded = value
    ref[at, a + 1] = rounded
    if a == 2:
        rolled = pltpu.roll(value[ROWS - SUB :].astype(F32), 1, 0).astype(BF)
        ref[at, 0, 0:SUB] = rolled * masks[0, 0:SUB]
        for t in range(1, TILES):
            low = t * SUB
            ref[at, 0, low : low + SUB] = rounded[low - SUB : low] * masks[0, low : low + SUB]
    if a == 0:
        for t in range(TILES - 1):
            low = t * SUB
            ref[at, 4, low : low + SUB] = (
                rounded[low + SUB : low + 2 * SUB] * masks[1, low : low + SUB]
            )
        rolled = pltpu.roll(value[:SUB].astype(F32), SUB - 1, 0).astype(BF)
        ref[at, 4, ROWS - SUB :] = rolled * masks[1, ROWS - SUB :]


def widen(weight_ref):
    channels = weight_ref.shape[-1]
    taps = weight_ref[...].reshape(-1, channels)
    row, lane = iota((channels, LANES), 0), iota((channels, LANES), 1)
    halves = []
    for shift in (0, channels):
        wide = dot(taps, (lane == row + shift).astype(BF)) * 0.5
        wide = wide.astype(BF)
        halves.append(
            [
                [wide[(p * 3 + q) * channels : (p * 3 + q + 1) * channels] for q in range(3)]
                for p in range(3)
            ]
        )
    return halves


def build_conv(weight_ref, w_pair, w_one, layer):
    low, high = widen(weight_ref)
    if layer == 1:
        low, high = high, low
    zero = jnp.zeros((256, LANES), BF)
    blocks = [
        jnp.concatenate(
            [low[p][0], low[p][1] + high[p][0], low[p][2] + high[p][1], high[p][2]], axis=0
        )
        for p in range(3)
    ]
    for i in range(4):
        at = slice(i * 256, (i + 1) * 256)
        w_pair[layer, at, 0:LANES] = blocks[i] if i < 3 else zero
        w_pair[layer, at, LANES:] = blocks[i - 1] if i > 0 else zero
    for i in range(3):
        w_one[layer, i * 256 : (i + 1) * 256, :] = blocks[i]


def build_up(weight_ref, w_up):
    low, high = widen(weight_ref)
    zero = jnp.zeros((64, LANES), BF)
    for a in range(3):
        first = [low[a][0] + high[a][1], low[a][2], zero]
        second = [zero, high[a][0], low[a][1] + high[a][2]]
        for n in range(3):
            at = slice((3 * a + n) * LANES, (3 * a + n + 1) * LANES)
            w_up[0:64, at] = first[n]
            w_up[64:128, at] = second[n]


def build_head(weight_ref, w_head):
    fields = weight_ref.shape[0]
    row, lane = iota((fields, LANES), 0), iota((fields, LANES), 1)
    tiled = lax.dot_general(
        weight_ref[...],
        (lane % fields == row).astype(BF),
        (((0,), (0,)), ((), ())),
        preferred_element_type=F32,
    )
    pixel = iota(tiled.shape, 1) // fields
    for p in range(16):
        for part, v in enumerate((1, 0)):
            block = jnp.where(pixel == 2 * p + v, tiled, 0.0).astype(BF)
            at = p * LANES + part * 64
            w_head[at : at + 64, :] = block


def conv(ref, w_pair, w_one, bias, layer, at, count):
    pieces = [
        [ref[pl.ds(at + d, count), i].reshape(count * ROWS, LANES) for d in range(2)]
        for i in range(5)
    ]
    both = dot(jnp.concatenate(sum(pieces[:4], []), axis=1), w_pair[layer])
    last = dot(jnp.concatenate(sum(pieces[2:], []), axis=1), w_one[layer])
    rows = [both[:, :LANES], both[:, LANES:], last]
    return [gelu_of_half(z + bias) for z in rows]


def kernel(
    lat_count,
    lon_count,
    x_ref,
    ocean_ref,
    band_ref,
    up_weight,
    up_bias,
    first_weight,
    first_bias,
    second_weight,
    second_bias,
    head_weight,
    head_bias,
    out_ref,
    edge,
    halo,
    corner,
    side,
    xc,
    zero_layer,
    one_layer,
    grown,
    w_up,
    w_pair,
    w_one,
    w_head,
    masks,
    spread,
    gather,
    outgoing,
    incoming,
    halo_send,
    halo_recv,
    out_send,
    out_recv,
):
    me = lax.axis_index("lat")
    lon = lax.axis_index("lon")
    north, south = (me + lat_count - 1) % lat_count, (me + 1) % lat_count
    west, east = (lon + lon_count - 1) % lon_count, (lon + 1) % lon_count
    width = x_ref.shape[1]

    barrier = pltpu.get_barrier_semaphore()

    def greet(t, carry):
        pl.semaphore_signal(
            barrier,
            inc=1,
            device_id={"lat": (me + t) % lat_count, "lon": lon},
            device_id_type=MESH,
        )
        return carry

    lax.fori_loop(1, lat_count, greet, 0)
    others = [(me, west), (me, east)] + [(r, c) for r in (north, south) for c in (west, east)]
    for r, c in others:
        pl.semaphore_signal(
            barrier, inc=1, device_id={"lat": r, "lon": c}, device_id_type=MESH
        )

    build_up(up_weight, w_up)
    build_conv(first_weight, w_pair, w_one, 0)
    build_conv(second_weight, w_pair, w_one, 1)
    build_head(head_weight, w_head)

    edge[0] = x_ref[0:SUB, :].astype(F32)[0:1]
    edge[1] = x_ref[ROWS - SUB :, :].astype(F32)[SUB - 1 :]

    pl.semaphore_wait(barrier, lat_count - 1 + len(others))
    first, final = pl.ds(0, LANES), pl.ds(width - LANES, LANES)
    plan = [
        (edge.at[0], halo.at[1], north, lon),
        (edge.at[1], halo.at[0], south, lon),
        (x_ref.at[:, first], side.at[0], me, west),
        (x_ref.at[:, final], side.at[1], me, east),
        (edge.at[0, :, first], corner.at[1, 0], north, west),
        (edge.at[0, :, final], corner.at[1, 1], north, east),
        (edge.at[1, :, first], corner.at[0, 0], south, west),
        (edge.at[1, :, final], corner.at[0, 1], south, east),
    ]
    copies = []
    for n, (source, target, r, c) in enumerate(plan):
        copy = pltpu.make_async_remote_copy(
            src_ref=source,
            dst_ref=target,
            send_sem=halo_send.at[n],
            recv_sem=halo_recv.at[n],
            device_id={"lat": r, "lon": c},
            device_id_type=MESH,
        )
        copy.start()
        copies.append(copy)

    row, col = iota((ROWS, ROWS), 0), iota((ROWS, ROWS), 1)
    source = iota((LANES, ROWS), 0) == (me % 2) * ROWS + iota((LANES, ROWS), 1)
    source = source.astype(BF)
    ocean_all = ocean_ref[...].astype(F32).astype(BF)
    band_all = band_ref[...].astype(F32).astype(BF)
    half_rows = ocean_all.shape[0]
    mine = (iota((SUB, half_rows), 1) == me // 2).astype(BF)
    ocean_row = dot(dot(mine, ocean_all).astype(BF), source)[0:1]
    band_row = dot(dot(mine, band_all).astype(BF), source)[0:1]
    eye = (row == col).astype(F32)
    before = (row < col).astype(F32)
    ocean_col = jnp.sum(eye * ocean_row, axis=1, keepdims=True)
    band_col = jnp.sum(eye * band_row, axis=1, keepdims=True)
    order_row = jnp.sum(before * ocean_col, axis=0, keepdims=True) + 1.0
    order_col = jnp.sum((col < row).astype(F32) * ocean_row, axis=1, keepdims=True) + 1.0
    total = jnp.sum(ocean_row, axis=1, keepdims=True)
    place = place_of(row).astype(F32)
    pick = jnp.where(place == order_row, ocean_row, 0.0)
    top = (place[:, 0:1] == 0.0).astype(F32)
    bottom = (place[:, 0:1] == total + 1.0).astype(F32)
    has_north = jnp.where(me > 0, 1.0, 0.0)
    has_south = jnp.where(me < lat_count - 1, 1.0, 0.0)
    above = jnp.sum((row + 1 == col).astype(F32) * ocean_col, axis=0, keepdims=True)
    above = above + jnp.where(col[0:1] == 0, has_north, 0.0)
    below = jnp.sum((row == col + 1).astype(F32) * ocean_col, axis=0, keepdims=True)
    below = below + jnp.where(col[0:1] == ROWS - 1, has_south, 0.0)
    up_mask = jnp.sum(pick * above, axis=1, keepdims=True) + bottom
    down_mask = jnp.sum(pick * below, axis=1, keepdims=True) + top
    masks[0] = jnp.broadcast_to(up_mask, (ROWS, LANES)).astype(BF)
    masks[1] = jnp.broadcast_to(down_mask, (ROWS, LANES)).astype(BF)

    earlier = jnp.where(band_col == band_row, before, 0.0) * ocean_col
    turn_row = jnp.sum(earlier, axis=0, keepdims=True)
    line = iota((lat_count * SENT, ROWS), 0)
    slot = (line // SENT * MOST + line % MOST).astype(F32)
    leaves = jnp.where(slot == band_row * 2.0 + turn_row, ocean_row, 0.0).astype(BF)
    lane = iota((ROWS, 3 * ROWS), 1)
    there = place_of(lane % ROWS).astype(F32) == order_col
    there = jnp.where(there, ocean_col, 0.0).astype(BF)
    moved = dot(leaves, there)
    line, lane = iota(moved.shape, 0), iota(moved.shape, 1)
    spread[...] = jnp.where(line % SENT // MOST == lane // ROWS, moved, 0.0).astype(BF)

    arrive = jnp.where(band_all.astype(F32) == me.astype(F32), ocean_all.astype(F32), 0.0)
    width_in = lat_count * SENT
    home = iota((LANES, width_in), 1) // SENT
    counts = dot(arrive.astype(BF), (iota((LANES, width_in), 0) // ROWS == home % 2).astype(BF))
    home = iota(counts.shape, 1) // SENT
    count_row = jnp.sum(
        jnp.where(iota(counts.shape, 0) == home // 2, counts, 0.0), axis=0, keepdims=True
    )
    sooner = jnp.where(iota(counts.shape, 0) < home // 2, counts, 0.0)
    other = dot(arrive.astype(BF), (iota((LANES, width_in), 0) // ROWS != iota((LANES, width_in), 1) // SENT % 2).astype(BF))
    sooner = sooner + jnp.where(iota(counts.shape, 0) < home // 2, other, 0.0)
    sooner = sooner + jnp.where(
        (iota(counts.shape, 0) == home // 2) & (home % 2 == 1), other, 0.0
    )
    base_row = jnp.sum(sooner, axis=0, keepdims=True)
    slots = out_ref.shape[1]
    shape = (3 * slots, width_in)
    line, lane = iota(shape, 0), iota(shape, 1)
    turn = lane % MOST
    number = (line % slots - turn).astype(F32)
    hit = (number == base_row) & (turn.astype(F32) < count_row) & (lane % SENT // MOST == line // slots)
    gather[...] = jnp.where(hit, 1.0, 0.0).astype(BF)

    bias_up, bias_one, bias_two = (
        jnp.concatenate([b[...], b[...]], axis=1) * 0.5 for b in (up_bias, first_bias, second_bias)
    )
    bias_head = jnp.concatenate([head_bias[...]] * (LANES // head_bias.shape[1]), axis=1)

    for copy in copies[:2]:
        copy.wait_recv()

    ends = iota((ROWS, SUB), 1)
    pick_ends = jnp.where(ends == 0, top, jnp.where(ends == 1, bottom, 0.0))
    pick_all = jnp.concatenate([pick.astype(BF), pick_ends.astype(BF)], axis=1)

    def two_rows(upper, lower):
        which = iota((SUB, upper.shape[1]), 0)
        return jnp.where(which == 0, upper, jnp.where(which == 1, lower, 0.0)).astype(BF)

    lifted = dot(
        pick_all, jnp.concatenate([x_ref[...], two_rows(halo[0], halo[1])], axis=0)
    ).astype(BF)
    for j in range(PAIRS):
        xc[j] = lifted[:, j * LANES : (j + 1) * LANES]
    low_lanes = iota((1, LANES), 1) < 64

    def outer_columns():
        for copy in copies[2:]:
            copy.wait_recv()
        joined = jnp.where(low_lanes, side[0].astype(F32), side[1].astype(F32)).astype(BF)
        joined_ends = two_rows(
            jnp.where(low_lanes, corner[0, 0], corner[0, 1]),
            jnp.where(low_lanes, corner[1, 0], corner[1, 1]),
        )
        outer = dot(pick_all, jnp.concatenate([joined, joined_ends], axis=0)).astype(BF)
        z = dot(outer, w_up[...])
        for a in range(3):
            for n, at in ((2, 0), (0, 3 * PAIRS + 1)):
                grow = gelu_of_half(z[:, (3 * a + n) * LANES :][:, :LANES] + bias_up)
                store_layer(zero_layer, at, a, grow, masks)

    high = jnp.where(low_lanes, 0.0, 1.0).astype(BF)
    low = jnp.where(low_lanes, 1.0, 0.0).astype(BF)

    def lift(start, group):
        source = xc[pl.ds(start, group)].reshape(group * ROWS, LANES)
        z = dot(source, w_up[...])
        for a in range(3):
            for n in range(3):
                grow = gelu_of_half(z[:, (3 * a + n) * LANES :][:, :LANES] + bias_up)
                for j in range(group):
                    value = grow[j * ROWS : (j + 1) * ROWS]
                    store_layer(zero_layer, 3 * (start + j) + 1 + n, a, value, masks)

    def convolve(base, count):
        rows = conv(zero_layer, w_pair, w_one, bias_one, 0, base, count)
        for a in range(3):
            for j in range(count):
                store_layer(one_layer, base + j, a, rows[a][j * ROWS : (j + 1) * ROWS], masks)

    def finish(n):
        tile, tiles = PARTS[n]
        base = tile * WIDE
        rows = conv(one_layer, w_pair, w_one, bias_two, 1, base, tiles * WIDE)
        for a in range(3):
            for j in range(tiles * WIDE):
                skip = one_layer[base + j + 1, a + 1] * low + one_layer[base + j, a + 1] * high
                grown[j, a] = rows[a][j * ROWS : (j + 1) * ROWS] + skip

        pieces = []
        for p in range(WIDE):
            made = [grown[i * WIDE + p].reshape(3 * ROWS, LANES) for i in range(tiles)]
            pieces.append(jnp.concatenate(made, axis=0))
        fields = dot(jnp.concatenate(pieces, axis=1), w_head[...])
        fields = (fields + bias_head).astype(BF)
        for i in range(tiles):
            sent = dot(spread[...], fields[i * 3 * ROWS : (i + 1) * 3 * ROWS]).astype(BF)
            outgoing[tile + i] = sent.reshape(lat_count, 3, MOST, LANES)

        def send(t, carry):
            target = (me + t) % lat_count
            pltpu.make_async_remote_copy(
                src_ref=outgoing.at[pl.ds(tile, tiles), target],
                dst_ref=incoming.at[pl.ds(tile, tiles), me],
                send_sem=out_send.at[n],
                recv_sem=out_recv.at[n],
                device_id={"lat": target, "lon": lon},
                device_id_type=MESH,
            ).start()
            return carry

        lax.fori_loop(1, lat_count, send, 0)
        for i in range(tiles):
            incoming[tile + i, me] = outgoing[tile + i, me]

    lift(10, 17)
    convolve(32, 49)
    finish(0)
    outer_columns()
    lift(0, 10)
    convolve(0, 32)
    finish(1)
    lift(27, 5)
    convolve(81, 16)
    finish(2)

    rest = pl.ds(0, lat_count - 1)
    for n, (tile, tiles) in enumerate(PARTS):
        block = incoming.at[pl.ds(tile, tiles), rest]
        pltpu.make_async_copy(block, block, out_recv.at[n]).wait()
        for i in range(tiles):
            landed = incoming[tile + i].reshape(lat_count * SENT, LANES)
            made = dot(gather[...], landed)
            for a in range(3):
                at = pl.ds((tile + i) * LANES, LANES)
                out_ref[a, :, at] = made[a * slots : (a + 1) * slots].astype(BF)
    for copy in copies:
        copy.wait_send()
    for n, (tile, tiles) in enumerate(PARTS):
        block = outgoing.at[pl.ds(tile, tiles), rest]
        pltpu.make_async_copy(block, block, out_send.at[n]).wait()


def body(lat_count, lon_count, coarse, ocean_mask, band_plan, up_weight, up_bias, first_weight,
         first_bias, second_weight, second_bias, head_weight, head_bias):
    slots = 32
    vmem = pl.BlockSpec(memory_space=pltpu.VMEM)
    row = lambda v: v.reshape(1, -1)
    made = pl.pallas_call(
        partial(kernel, lat_count, lon_count),
        out_shape=jax.ShapeDtypeStruct((3, slots, 768), BF),
        in_specs=[vmem] * 11,
        out_specs=vmem,
        scratch_shapes=[
            pltpu.VMEM((2, 1, coarse.shape[1]), F32),
            pltpu.VMEM((2, 1, coarse.shape[1]), F32),
            pltpu.VMEM((2, 2, 1, LANES), F32),
            pltpu.VMEM((2, ROWS, LANES), BF),
            pltpu.VMEM((PAIRS, ROWS, LANES), BF),
            pltpu.VMEM((3 * PAIRS + 2, 5, ROWS, LANES), BF),
            pltpu.VMEM((3 * PAIRS + 1, 5, ROWS, LANES), BF),
            pltpu.VMEM((3 * WIDE, 3, ROWS, LANES), BF),
            pltpu.VMEM((LANES, 9 * LANES), BF),
            pltpu.VMEM((2, 1024, 2 * LANES), BF),
            pltpu.VMEM((2, 768, LANES), BF),
            pltpu.VMEM((16 * LANES, LANES), BF),
            pltpu.VMEM((2, ROWS, LANES), BF),
            pltpu.VMEM((lat_count * SENT, 3 * ROWS), BF),
            pltpu.VMEM((3 * slots, lat_count * SENT), BF),
            pltpu.VMEM((6, lat_count, 3, MOST, LANES), BF),
            pltpu.VMEM((6, lat_count, 3, MOST, LANES), BF),
            pltpu.SemaphoreType.DMA((8,)),
            pltpu.SemaphoreType.DMA((8,)),
            pltpu.SemaphoreType.DMA((len(PARTS),)),
            pltpu.SemaphoreType.DMA((len(PARTS),)),
        ],
        compiler_params=pltpu.CompilerParams(
            collective_id=0, has_side_effects=True, vmem_limit_bytes=60 * 2**20
        ),
    )(
        coarse,
        ocean_mask.reshape(-1, LANES),
        band_plan.reshape(-1, LANES),
        up_weight,
        row(up_bias),
        first_weight,
        row(first_bias),
        second_weight,
        row(second_bias),
        head_weight.T,
        row(head_bias),
    )
    return made.transpose(1, 0, 2).astype(F32)


def solution(mesh):
    in_specs = (P("lat", "lon"), P(), P(), P(), P(), P(), P(), P(), P(), P(), P())
    out_specs = P("lat", None, "lon")
    call = partial(body, mesh.shape["lat"], mesh.shape["lon"])
    return jax.shard_map(call, mesh=mesh, in_specs=in_specs, out_specs=out_specs, check_vma=False)
```

```python
from functools import partial

import jax
import jax.numpy as jnp
import numpy as np
from jax import lax
from jax.experimental import pallas as pl
from jax.experimental.pallas import tpu as pltpu
from jax.sharding import PartitionSpec as P

MESH = pl.DeviceIdType.MESH
BF = jnp.bfloat16
F32 = jnp.float32
ROWS = 64
SENT = 6
MOST = 2
WIDE = 16
SUB = 16
TILES = ROWS // SUB
LANES = 128
PAIRS = 32
RING = 4
SLOPE = float(np.sqrt(2.0 / np.pi))


def dot(a, b):
    return jnp.dot(a, b, preferred_element_type=F32)


def dot_t(a, b):
    return lax.dot_general(a, b, (((1,), (1,)), ((), ())), preferred_element_type=F32)


def iota(shape, dim):
    return lax.broadcasted_iota(jnp.int32, shape, dim)


def gelu_of_half(h):
    h = h.astype(BF)
    return h + h * jnp.tanh(h * (BF(2 * SLOPE) + BF(8 * 0.044715 * SLOPE) * (h * h)))


def place_of(m):
    return (m % SUB) * TILES + m // SUB


def store_layer(ref, at, a, value, masks):
    rounded = value
    ref[at, a + 1] = rounded
    if a == 2:
        rolled = pltpu.roll(value[ROWS - SUB :].astype(F32), 1, 0).astype(BF)
        ref[at, 0, 0:SUB] = rolled * masks[0, 0:SUB]
        for t in range(1, TILES):
            low = t * SUB
            ref[at, 0, low : low + SUB] = rounded[low - SUB : low] * masks[0, low : low + SUB]
    if a == 0:
        for t in range(TILES - 1):
            low = t * SUB
            ref[at, 4, low : low + SUB] = (
                rounded[low + SUB : low + 2 * SUB] * masks[1, low : low + SUB]
            )
        rolled = pltpu.roll(value[:SUB].astype(F32), SUB - 1, 0).astype(BF)
        ref[at, 4, ROWS - SUB :] = rolled * masks[1, ROWS - SUB :]


def widen(weight_ref):
    channels = weight_ref.shape[-1]
    taps = weight_ref[...].reshape(-1, channels)
    row, lane = iota((channels, LANES), 0), iota((channels, LANES), 1)
    halves = []
    for shift in (0, channels):
        wide = dot(taps, (lane == row + shift).astype(BF)) * 0.5
        wide = wide.astype(BF)
        halves.append(
            [
                [wide[(p * 3 + q) * channels : (p * 3 + q + 1) * channels] for q in range(3)]
                for p in range(3)
            ]
        )
    return halves


def build_conv(weight_ref, w_pair, w_one, layer):
    low, high = widen(weight_ref)
    if layer == 1:
        low, high = high, low
    zero = jnp.zeros((256, LANES), BF)
    blocks = [
        jnp.concatenate(
            [low[p][0], low[p][1] + high[p][0], low[p][2] + high[p][1], high[p][2]], axis=0
        )
        for p in range(3)
    ]
    for i in range(4):
        at = slice(i * 256, (i + 1) * 256)
        w_pair[layer, at, 0:LANES] = blocks[i] if i < 3 else zero
        w_pair[layer, at, LANES:] = blocks[i - 1] if i > 0 else zero
    for i in range(3):
        w_one[layer, i * 256 : (i + 1) * 256, :] = blocks[i]


def build_up(weight_ref, w_up):
    low, high = widen(weight_ref)
    zero = jnp.zeros((64, LANES), BF)
    for a in range(3):
        first = [low[a][0] + high[a][1], low[a][2], zero]
        second = [zero, high[a][0], low[a][1] + high[a][2]]
        for n in range(3):
            at = slice((3 * a + n) * LANES, (3 * a + n + 1) * LANES)
            w_up[0:64, at] = first[n]
            w_up[64:128, at] = second[n]


def build_head(weight_ref, w_head):
    fields = weight_ref.shape[0]
    row, lane = iota((fields, LANES), 0), iota((fields, LANES), 1)
    tiled = lax.dot_general(
        weight_ref[...],
        (lane % fields == row).astype(BF),
        (((0,), (0,)), ((), ())),
        preferred_element_type=F32,
    )
    pixel = iota(tiled.shape, 1) // fields
    for p in range(16):
        for part, v in enumerate((1, 0)):
            block = jnp.where(pixel == 2 * p + v, tiled, 0.0).astype(BF)
            at = p * LANES + part * 64
            w_head[at : at + 64, :] = block


def conv(ref, w_pair, w_one, bias, layer, places):
    def stack(i, d):
        if isinstance(places, range):
            return ref[places.start + d : places.stop + d, i].reshape(len(places) * ROWS, LANES)
        return jnp.concatenate([ref[at + d, i] for at in places], axis=0)

    pieces = [[stack(i, d) for d in range(2)] for i in range(5)]
    both = dot(jnp.concatenate(sum(pieces[:4], []), axis=1), w_pair[layer])
    last = dot(jnp.concatenate(sum(pieces[2:], []), axis=1), w_one[layer])
    rows = [both[:, :LANES], both[:, LANES:], last]
    return [gelu_of_half(z + bias) for z in rows]


def prepare(
    lat_count, x_hbm, ocean_ref, band_ref, ends_ref, pick_out, masks, spread, gather,
    rows, edge, halo, load, halo_send, halo_recv,
):
    me = lax.axis_index("lat")
    lon = lax.axis_index("lon")
    north, south = (me + lat_count - 1) % lat_count, (me + 1) % lat_count
    barrier = pltpu.get_barrier_semaphore()
    for r in (north, south):
        pl.semaphore_signal(barrier, inc=1, device_id={"lat": r, "lon": lon}, device_id_type=MESH)
    loads = [
        pltpu.make_async_copy(x_hbm.at[pl.ds(low, SUB), :], rows.at[n], load.at[n])
        for n, low in enumerate((0, ROWS - SUB))
    ]
    for copy in loads:
        copy.start()
    for copy in loads:
        copy.wait()
    edge[0] = rows[0].astype(F32)[0:1]
    edge[1] = rows[1].astype(F32)[SUB - 1 :]
    pl.semaphore_wait(barrier, 2)
    copies = []
    for n, r in enumerate((north, south)):
        copy = pltpu.make_async_remote_copy(
            src_ref=edge.at[n],
            dst_ref=halo.at[1 - n],
            send_sem=halo_send.at[n],
            recv_sem=halo_recv.at[n],
            device_id={"lat": r, "lon": lon},
            device_id_type=MESH,
        )
        copy.start()
        copies.append(copy)

    row, col = iota((ROWS, ROWS), 0), iota((ROWS, ROWS), 1)
    source = iota((LANES, ROWS), 0) == (me % 2) * ROWS + iota((LANES, ROWS), 1)
    source = source.astype(BF)
    ocean_all = ocean_ref[...].astype(F32).astype(BF)
    band_all = band_ref[...].astype(F32).astype(BF)
    half_rows = ocean_all.shape[0]
    mine = (iota((SUB, half_rows), 1) == me // 2).astype(BF)
    ocean_row = dot(dot(mine, ocean_all).astype(BF), source)[0:1]
    band_row = dot(dot(mine, band_all).astype(BF), source)[0:1]
    eye = (row == col).astype(F32)
    before = (row < col).astype(F32)
    ocean_col = jnp.sum(eye * ocean_row, axis=1, keepdims=True)
    band_col = jnp.sum(eye * band_row, axis=1, keepdims=True)
    order_row = jnp.sum(before * ocean_col, axis=0, keepdims=True) + 1.0
    order_col = jnp.sum((col < row).astype(F32) * ocean_row, axis=1, keepdims=True) + 1.0
    total = jnp.sum(ocean_row, axis=1, keepdims=True)
    place = place_of(row).astype(F32)
    pick = jnp.where(place == order_row, ocean_row, 0.0)
    top = (place[:, 0:1] == 0.0).astype(F32)
    bottom = (place[:, 0:1] == total + 1.0).astype(F32)
    has_north = jnp.where(me > 0, 1.0, 0.0)
    has_south = jnp.where(me < lat_count - 1, 1.0, 0.0)
    above = jnp.sum((row + 1 == col).astype(F32) * ocean_col, axis=0, keepdims=True)
    above = above + jnp.where(col[0:1] == 0, has_north, 0.0)
    below = jnp.sum((row == col + 1).astype(F32) * ocean_col, axis=0, keepdims=True)
    below = below + jnp.where(col[0:1] == ROWS - 1, has_south, 0.0)
    up_mask = jnp.sum(pick * above, axis=1, keepdims=True) + bottom
    down_mask = jnp.sum(pick * below, axis=1, keepdims=True) + top
    masks[0] = jnp.broadcast_to(up_mask, (ROWS, LANES)).astype(BF)
    masks[1] = jnp.broadcast_to(down_mask, (ROWS, LANES)).astype(BF)

    earlier = jnp.where(band_col == band_row, before, 0.0) * ocean_col
    turn_row = jnp.sum(earlier, axis=0, keepdims=True)
    line = iota((lat_count * SENT, ROWS), 0)
    slot = (line // SENT * MOST + line % MOST).astype(F32)
    leaves = jnp.where(slot == band_row * 2.0 + turn_row, ocean_row, 0.0).astype(BF)
    lane = iota((ROWS, 3 * ROWS), 1)
    there = place_of(lane % ROWS).astype(F32) == order_col
    there = jnp.where(there, ocean_col, 0.0).astype(BF)
    moved = dot(leaves, there)
    line, lane = iota(moved.shape, 0), iota(moved.shape, 1)
    spread[...] = jnp.where(line % SENT // MOST == lane // ROWS, moved, 0.0).astype(BF)

    arrive = jnp.where(band_all.astype(F32) == me.astype(F32), ocean_all.astype(F32), 0.0)
    width_in = lat_count * SENT
    home = iota((LANES, width_in), 1) // SENT
    counts = dot(arrive.astype(BF), (iota((LANES, width_in), 0) // ROWS == home % 2).astype(BF))
    home = iota(counts.shape, 1) // SENT
    count_row = jnp.sum(
        jnp.where(iota(counts.shape, 0) == home // 2, counts, 0.0), axis=0, keepdims=True
    )
    sooner = jnp.where(iota(counts.shape, 0) < home // 2, counts, 0.0)
    other = dot(arrive.astype(BF), (iota((LANES, width_in), 0) // ROWS != iota((LANES, width_in), 1) // SENT % 2).astype(BF))
    sooner = sooner + jnp.where(iota(counts.shape, 0) < home // 2, other, 0.0)
    sooner = sooner + jnp.where(
        (iota(counts.shape, 0) == home // 2) & (home % 2 == 1), other, 0.0
    )
    base_row = jnp.sum(sooner, axis=0, keepdims=True)
    slots = gather.shape[0] // 3
    shape = (3 * slots, width_in)
    line, lane = iota(shape, 0), iota(shape, 1)
    turn = lane % MOST
    number = (line % slots - turn).astype(F32)
    hit = (number == base_row) & (turn.astype(F32) < count_row) & (lane % SENT // MOST == line // slots)
    gather[...] = jnp.where(hit, 1.0, 0.0).astype(BF)

    ends = iota((ROWS, SUB), 1)
    pick_ends = jnp.where(ends == 0, top, jnp.where(ends == 1, bottom, 0.0))
    pick_out[...] = jnp.concatenate([pick.astype(BF), pick_ends.astype(BF)], axis=1)

    for copy in copies:
        copy.wait_recv()
    ends_ref[...] = halo[...]
    for copy in copies:
        copy.wait_send()


def kernel(
    lat_count,
    lon_count,
    x_ref,
    ends_ref,
    pick_ref,
    masks,
    spread,
    gather,
    up_weight,
    up_bias,
    first_weight,
    first_bias,
    second_weight,
    second_bias,
    head_weight,
    head_bias,
    out_ref,
    edge,
    corner,
    side,
    xc,
    zero_layer,
    one_layer,
    grown,
    w_up,
    w_pair,
    w_one,
    w_head,
    outgoing,
    incoming,
    halo_send,
    halo_recv,
    out_send,
    out_recv,
):
    me = lax.axis_index("lat")
    lon = lax.axis_index("lon")
    north, south = (me + lat_count - 1) % lat_count, (me + 1) % lat_count
    west, east = (lon + lon_count - 1) % lon_count, (lon + 1) % lon_count
    width = x_ref.shape[1]
    slots = out_ref.shape[1]

    barrier = pltpu.get_barrier_semaphore()
    others = [(me, west), (me, east)] + [(r, c) for r in (north, south) for c in (west, east)]
    for r, c in others:
        pl.semaphore_signal(
            barrier, inc=1, device_id={"lat": r, "lon": c}, device_id_type=MESH
        )

    def greet(t, carry):
        pl.semaphore_signal(
            barrier,
            inc=1,
            device_id={"lat": (me + t) % lat_count, "lon": lon},
            device_id_type=MESH,
        )
        return carry

    lax.fori_loop(1, lat_count, greet, 0)

    build_up(up_weight, w_up)
    build_conv(first_weight, w_pair, w_one, 0)
    build_conv(second_weight, w_pair, w_one, 1)
    build_head(head_weight, w_head)
    bias_up, bias_one, bias_two = (
        jnp.concatenate([b[...], b[...]], axis=1) * 0.5 for b in (up_bias, first_bias, second_bias)
    )
    bias_head = jnp.concatenate([head_bias[...]] * (LANES // head_bias.shape[1]), axis=1)

    edge[0] = x_ref[0:SUB, :].astype(F32)[0:1]
    edge[1] = x_ref[ROWS - SUB :, :].astype(F32)[SUB - 1 :]

    pick_all = pick_ref[...]

    def two_rows(upper, lower):
        which = iota((SUB, upper.shape[1]), 0)
        return jnp.where(which == 0, upper, jnp.where(which == 1, lower, 0.0)).astype(BF)

    lifted = dot(
        pick_all, jnp.concatenate([x_ref[...], two_rows(ends_ref[0], ends_ref[1])], axis=0)
    ).astype(BF)
    for j in range(PAIRS):
        xc[j] = lifted[:, j * LANES : (j + 1) * LANES]
    low_lanes = iota((1, LANES), 1) < 64
    high = jnp.where(low_lanes, 0.0, 1.0).astype(BF)
    low = jnp.where(low_lanes, 1.0, 0.0).astype(BF)

    def lift(start, group):
        source = xc[pl.ds(start, group)].reshape(group * ROWS, LANES)
        z = dot(source, w_up[...])
        for a in range(3):
            for n in range(3):
                grow = gelu_of_half(z[:, (3 * a + n) * LANES :][:, :LANES] + bias_up)
                for j in range(group):
                    value = grow[j * ROWS : (j + 1) * ROWS]
                    store_layer(zero_layer, 3 * (start + j) + 1 + n, a, value, masks)

    lift(0, PAIRS // 2)

    pl.semaphore_wait(barrier, lat_count - 1 + len(others))
    first, final = pl.ds(0, LANES), pl.ds(width - LANES, LANES)
    plan = [
        (x_ref.at[:, first], side.at[0], me, west),
        (x_ref.at[:, final], side.at[1], me, east),
        (edge.at[0, :, first], corner.at[1, 0], north, west),
        (edge.at[0, :, final], corner.at[1, 1], north, east),
        (edge.at[1, :, first], corner.at[0, 0], south, west),
        (edge.at[1, :, final], corner.at[0, 1], south, east),
    ]
    copies = []
    for n, (source, target, r, c) in enumerate(plan):
        copy = pltpu.make_async_remote_copy(
            src_ref=source,
            dst_ref=target,
            send_sem=halo_send.at[n],
            recv_sem=halo_recv.at[n],
            device_id={"lat": r, "lon": c},
            device_id_type=MESH,
        )
        copy.start()
        copies.append(copy)

    def convolve(places):
        rows = conv(zero_layer, w_pair, w_one, bias_one, 0, places)
        for a in range(3):
            for j, at in enumerate(places):
                store_layer(one_layer, at, a, rows[a][j * ROWS : (j + 1) * ROWS], masks)

    lift(PAIRS // 2, PAIRS // 2)
    convolve(range(1, 3 * PAIRS // 2 + 1))
    convolve(range(3 * PAIRS // 2 + 1, 3 * PAIRS))

    for copy in copies:
        copy.wait_recv()
    joined = jnp.where(low_lanes, side[0].astype(F32), side[1].astype(F32)).astype(BF)
    joined_ends = two_rows(
        jnp.where(low_lanes, corner[0, 0], corner[0, 1]),
        jnp.where(low_lanes, corner[1, 0], corner[1, 1]),
    )
    outer = dot(pick_all, jnp.concatenate([joined, joined_ends], axis=0)).astype(BF)
    z = dot(outer, w_up[...])
    for a in range(3):
        for n, at in ((2, 0), (0, 3 * PAIRS + 1)):
            grow = gelu_of_half(z[:, (3 * a + n) * LANES :][:, :LANES] + bias_up)
            store_layer(zero_layer, at, a, grow, masks)
    convolve((0, 3 * PAIRS))

    for half in range(2):
        base = half * 3 * WIDE
        rows = conv(one_layer, w_pair, w_one, bias_two, 1, range(base, base + 3 * WIDE))
        for a in range(3):
            for j in range(3 * WIDE):
                skip = one_layer[base + j + 1, a + 1] * low + one_layer[base + j, a + 1] * high
                grown[j, a] = rows[a][j * ROWS : (j + 1) * ROWS] + skip
        pieces = []
        for p in range(WIDE):
            made = [grown[i * WIDE + p].reshape(3 * ROWS, LANES) for i in range(3)]
            pieces.append(jnp.concatenate(made, axis=0))
        fields = dot(jnp.concatenate(pieces, axis=1), w_head[...])
        fields = (fields + bias_head).astype(BF)
        for i in range(3):
            sent = dot(spread[...], fields[i * 3 * ROWS : (i + 1) * 3 * ROWS]).astype(BF)
            outgoing[:, half * 3 + i] = sent.reshape(lat_count, 3, MOST, LANES)

    runs = lat_count // RING
    side_of = me // RING // (runs // 2)

    def send(i, carry):
        run = i * side_of + (runs - 1 - i) * (1 - side_of)
        for x in range(RING):
            target = run * RING + x

            @pl.when(target != me)
            def _():
                pltpu.make_async_remote_copy(
                    src_ref=outgoing.at[target],
                    dst_ref=incoming.at[me],
                    send_sem=out_send,
                    recv_sem=out_recv,
                    device_id={"lat": target, "lon": lon},
                    device_id_type=MESH,
                ).start()

        return carry

    lax.fori_loop(0, runs, send, 0)
    incoming[me] = outgoing[me]

    rest = pl.ds(0, lat_count - 1)
    pltpu.make_async_copy(incoming.at[rest], incoming.at[rest], out_recv).wait()
    for i in range(6):
        landed = incoming[:, i].reshape(lat_count * SENT, LANES)
        made = dot(gather[...], landed).astype(BF)
        for a in range(3):
            out_ref[a, :, i * LANES : (i + 1) * LANES] = made[a * slots : (a + 1) * slots]
    for copy in copies:
        copy.wait_send()
    pltpu.make_async_copy(outgoing.at[rest], outgoing.at[rest], out_send).wait()


def body(lat_count, lon_count, coarse, ocean_mask, band_plan, up_weight, up_bias, first_weight,
         first_bias, second_weight, second_bias, head_weight, head_bias):
    slots = 32
    width = coarse.shape[1]
    vmem = pl.BlockSpec(memory_space=pltpu.VMEM)
    row = lambda v: v.reshape(1, -1)
    prepared = pl.pallas_call(
        partial(prepare, lat_count),
        out_shape=(
            jax.ShapeDtypeStruct((2, 1, width), F32),
            jax.ShapeDtypeStruct((ROWS, ROWS + SUB), BF),
            jax.ShapeDtypeStruct((2, ROWS, LANES), BF),
            jax.ShapeDtypeStruct((lat_count * SENT, 3 * ROWS), BF),
            jax.ShapeDtypeStruct((3 * slots, lat_count * SENT), BF),
        ),
        in_specs=[pl.BlockSpec(memory_space=pl.ANY), vmem, vmem],
        out_specs=(vmem,) * 5,
        scratch_shapes=[
            pltpu.VMEM((2, SUB, width), BF),
            pltpu.VMEM((2, 1, width), F32),
            pltpu.VMEM((2, 1, width), F32),
            pltpu.SemaphoreType.DMA((2,)),
            pltpu.SemaphoreType.DMA((2,)),
            pltpu.SemaphoreType.DMA((2,)),
        ],
        compiler_params=pltpu.CompilerParams(collective_id=0, has_side_effects=True),
    )(coarse, ocean_mask.reshape(-1, LANES), band_plan.reshape(-1, LANES))
    made = pl.pallas_call(
        partial(kernel, lat_count, lon_count),
        out_shape=jax.ShapeDtypeStruct((3, slots, 768), BF),
        in_specs=[vmem] * 14,
        out_specs=vmem,
        scratch_shapes=[
            pltpu.VMEM((2, 1, width), F32),
            pltpu.VMEM((2, 2, 1, LANES), F32),
            pltpu.VMEM((2, ROWS, LANES), BF),
            pltpu.VMEM((PAIRS, ROWS, LANES), BF),
            pltpu.VMEM((3 * PAIRS + 2, 5, ROWS, LANES), BF),
            pltpu.VMEM((3 * PAIRS + 1, 5, ROWS, LANES), BF),
            pltpu.VMEM((3 * WIDE, 3, ROWS, LANES), BF),
            pltpu.VMEM((LANES, 9 * LANES), BF),
            pltpu.VMEM((2, 1024, 2 * LANES), BF),
            pltpu.VMEM((2, 768, LANES), BF),
            pltpu.VMEM((16 * LANES, LANES), BF),
            pltpu.VMEM((lat_count, 6, 3, MOST, LANES), BF),
            pltpu.VMEM((lat_count, 6, 3, MOST, LANES), BF),
            pltpu.SemaphoreType.DMA((6,)),
            pltpu.SemaphoreType.DMA((6,)),
            pltpu.SemaphoreType.DMA,
            pltpu.SemaphoreType.DMA,
        ],
        compiler_params=pltpu.CompilerParams(
            collective_id=1, has_side_effects=True, vmem_limit_bytes=60 * 2**20
        ),
    )(
        coarse,
        *prepared,
        up_weight,
        row(up_bias),
        first_weight,
        row(first_bias),
        second_weight,
        row(second_bias),
        head_weight.T,
        row(head_bias),
    )
    return made.transpose(1, 0, 2).astype(F32)


def solution(mesh):
    in_specs = (P("lat", "lon"), P(), P(), P(), P(), P(), P(), P(), P(), P(), P())
    out_specs = P("lat", None, "lon")
    call = partial(body, mesh.shape["lat"], mesh.shape["lon"])
    return jax.shard_map(call, mesh=mesh, in_specs=in_specs, out_specs=out_specs, check_vma=False)
```

```python
from functools import partial

import jax
import jax.numpy as jnp
import numpy as np
from jax import lax
from jax.experimental import pallas as pl
from jax.experimental.pallas import tpu as pltpu
from jax.sharding import PartitionSpec as P

MESH = pl.DeviceIdType.MESH
BF = jnp.bfloat16
F32 = jnp.float32
ROWS = 64
SENT = 6
MOST = 2
WIDE = 16
SUB = 16
TILES = ROWS // SUB
LANES = 128
PAIRS = 32
SLOPE = float(np.sqrt(2.0 / np.pi))


def dot(a, b):
    return jnp.dot(a, b, preferred_element_type=F32)


def dot_t(a, b):
    return lax.dot_general(a, b, (((1,), (1,)), ((), ())), preferred_element_type=F32)


def iota(shape, dim):
    return lax.broadcasted_iota(jnp.int32, shape, dim)


def gelu_of_half(h):
    h = h.astype(BF)
    return h + h * jnp.tanh(h * (BF(2 * SLOPE) + BF(8 * 0.044715 * SLOPE) * (h * h)))


def place_of(m):
    return (m % SUB) * TILES + m // SUB


def store_layer(ref, at, a, value, masks):
    rounded = value
    ref[at, a + 1] = rounded
    if a == 2:
        rolled = pltpu.roll(value[ROWS - SUB :].astype(F32), 1, 0).astype(BF)
        ref[at, 0, 0:SUB] = rolled * masks[0, 0:SUB]
        for t in range(1, TILES):
            low = t * SUB
            ref[at, 0, low : low + SUB] = rounded[low - SUB : low] * masks[0, low : low + SUB]
    if a == 0:
        for t in range(TILES - 1):
            low = t * SUB
            ref[at, 4, low : low + SUB] = (
                rounded[low + SUB : low + 2 * SUB] * masks[1, low : low + SUB]
            )
        rolled = pltpu.roll(value[:SUB].astype(F32), SUB - 1, 0).astype(BF)
        ref[at, 4, ROWS - SUB :] = rolled * masks[1, ROWS - SUB :]


def widen(weight_ref):
    channels = weight_ref.shape[-1]
    taps = weight_ref[...].reshape(-1, channels)
    row, lane = iota((channels, LANES), 0), iota((channels, LANES), 1)
    halves = []
    for shift in (0, channels):
        wide = dot(taps, (lane == row + shift).astype(BF)) * 0.5
        wide = wide.astype(BF)
        halves.append(
            [
                [wide[(p * 3 + q) * channels : (p * 3 + q + 1) * channels] for q in range(3)]
                for p in range(3)
            ]
        )
    return halves


def build_conv(weight_ref, w_pair, w_one, layer):
    low, high = widen(weight_ref)
    if layer == 1:
        low, high = high, low
    zero = jnp.zeros((256, LANES), BF)
    blocks = [
        jnp.concatenate(
            [low[p][0], low[p][1] + high[p][0], low[p][2] + high[p][1], high[p][2]], axis=0
        )
        for p in range(3)
    ]
    for i in range(4):
        at = slice(i * 256, (i + 1) * 256)
        w_pair[layer, at, 0:LANES] = blocks[i] if i < 3 else zero
        w_pair[layer, at, LANES:] = blocks[i - 1] if i > 0 else zero
    for i in range(3):
        w_one[layer, i * 256 : (i + 1) * 256, :] = blocks[i]


def build_up(weight_ref, w_up):
    low, high = widen(weight_ref)
    zero = jnp.zeros((64, LANES), BF)
    for a in range(3):
        first = [low[a][0] + high[a][1], low[a][2], zero]
        second = [zero, high[a][0], low[a][1] + high[a][2]]
        for n in range(3):
            at = slice((3 * a + n) * LANES, (3 * a + n + 1) * LANES)
            w_up[0:64, at] = first[n]
            w_up[64:128, at] = second[n]


def build_head(weight_ref, w_head):
    fields = weight_ref.shape[0]
    row, lane = iota((fields, LANES), 0), iota((fields, LANES), 1)
    tiled = lax.dot_general(
        weight_ref[...],
        (lane % fields == row).astype(BF),
        (((0,), (0,)), ((), ())),
        preferred_element_type=F32,
    )
    pixel = iota(tiled.shape, 1) // fields
    for p in range(16):
        for part, v in enumerate((1, 0)):
            block = jnp.where(pixel == 2 * p + v, tiled, 0.0).astype(BF)
            at = p * LANES + part * 64
            w_head[at : at + 64, :] = block


def conv(ref, w_pair, w_one, bias, layer, places):
    pieces = [
        [
            ref[places.start + d : places.stop + d, i].reshape(len(places) * ROWS, LANES)
            for d in range(2)
        ]
        for i in range(5)
    ]
    both = dot(jnp.concatenate(sum(pieces[:4], []), axis=1), w_pair[layer])
    last = dot(jnp.concatenate(sum(pieces[2:], []), axis=1), w_one[layer])
    rows = [both[:, :LANES], both[:, LANES:], last]
    return [gelu_of_half(z + bias) for z in rows]


def kernel(
    lat_count,
    lon_count,
    x_ref,
    ocean_ref,
    band_ref,
    up_weight,
    up_bias,
    first_weight,
    first_bias,
    second_weight,
    second_bias,
    head_weight,
    head_bias,
    out_ref,
    edge,
    halo,
    corner,
    side,
    xc,
    zero_layer,
    one_layer,
    grown,
    w_up,
    w_pair,
    w_one,
    w_head,
    masks,
    spread,
    gather,
    outgoing,
    incoming,
    halo_send,
    halo_recv,
    out_send,
    out_recv,
):
    me = lax.axis_index("lat")
    lon = lax.axis_index("lon")
    north, south = (me + lat_count - 1) % lat_count, (me + 1) % lat_count
    west, east = (lon + lon_count - 1) % lon_count, (lon + 1) % lon_count
    width = x_ref.shape[1]
    barrier = pltpu.get_barrier_semaphore()
    others = [(me, west), (me, east)] + [(r, c) for r in (north, south) for c in (west, east)]
    for r, c in others:
        pl.semaphore_signal(
            barrier, inc=1, device_id={"lat": r, "lon": c}, device_id_type=MESH
        )

    def greet(t, carry):
        pl.semaphore_signal(
            barrier,
            inc=1,
            device_id={"lat": (me + t) % lat_count, "lon": lon},
            device_id_type=MESH,
        )
        return carry

    lax.fori_loop(1, lat_count, greet, 0)

    build_up(up_weight, w_up)
    build_conv(first_weight, w_pair, w_one, 0)
    build_conv(second_weight, w_pair, w_one, 1)
    build_head(head_weight, w_head)
    edge[0] = x_ref[0:SUB, :].astype(F32)[0:1]
    edge[1] = x_ref[ROWS - SUB :, :].astype(F32)[SUB - 1 :]

    pl.semaphore_wait(barrier, lat_count - 1 + len(others))
    first, final = pl.ds(0, LANES), pl.ds(width - LANES, LANES)
    plan = [
        (edge.at[0], halo.at[1], north, lon),
        (edge.at[1], halo.at[0], south, lon),
        (x_ref.at[:, first], side.at[0], me, west),
        (x_ref.at[:, final], side.at[1], me, east),
        (edge.at[0, :, first], corner.at[1, 0], north, west),
        (edge.at[0, :, final], corner.at[1, 1], north, east),
        (edge.at[1, :, first], corner.at[0, 0], south, west),
        (edge.at[1, :, final], corner.at[0, 1], south, east),
    ]
    copies = []
    for n, (source, target, r, c) in enumerate(plan):
        copy = pltpu.make_async_remote_copy(
            src_ref=source,
            dst_ref=target,
            send_sem=halo_send.at[n],
            recv_sem=halo_recv.at[n],
            device_id={"lat": r, "lon": c},
            device_id_type=MESH,
        )
        copy.start()
        copies.append(copy)

    row, col = iota((ROWS, ROWS), 0), iota((ROWS, ROWS), 1)
    source = iota((LANES, ROWS), 0) == (me % 2) * ROWS + iota((LANES, ROWS), 1)
    source = source.astype(BF)
    ocean_all = ocean_ref[...].astype(F32).astype(BF)
    band_all = band_ref[...].astype(F32).astype(BF)
    half_rows = ocean_all.shape[0]
    mine = (iota((SUB, half_rows), 1) == me // 2).astype(BF)
    ocean_row = dot(dot(mine, ocean_all).astype(BF), source)[0:1]
    band_row = dot(dot(mine, band_all).astype(BF), source)[0:1]
    eye = (row == col).astype(F32)
    before = (row < col).astype(F32)
    ocean_col = jnp.sum(eye * ocean_row, axis=1, keepdims=True)
    band_col = jnp.sum(eye * band_row, axis=1, keepdims=True)
    order_row = jnp.sum(before * ocean_col, axis=0, keepdims=True) + 1.0
    order_col = jnp.sum((col < row).astype(F32) * ocean_row, axis=1, keepdims=True) + 1.0
    total = jnp.sum(ocean_row, axis=1, keepdims=True)
    place = place_of(row).astype(F32)
    pick = jnp.where(place == order_row, ocean_row, 0.0)
    top = (place[:, 0:1] == 0.0).astype(F32)
    bottom = (place[:, 0:1] == total + 1.0).astype(F32)
    has_north = jnp.where(me > 0, 1.0, 0.0)
    has_south = jnp.where(me < lat_count - 1, 1.0, 0.0)
    above = jnp.sum((row + 1 == col).astype(F32) * ocean_col, axis=0, keepdims=True)
    above = above + jnp.where(col[0:1] == 0, has_north, 0.0)
    below = jnp.sum((row == col + 1).astype(F32) * ocean_col, axis=0, keepdims=True)
    below = below + jnp.where(col[0:1] == ROWS - 1, has_south, 0.0)
    up_mask = jnp.sum(pick * above, axis=1, keepdims=True) + bottom
    down_mask = jnp.sum(pick * below, axis=1, keepdims=True) + top
    masks[0] = jnp.broadcast_to(up_mask, (ROWS, LANES)).astype(BF)
    masks[1] = jnp.broadcast_to(down_mask, (ROWS, LANES)).astype(BF)

    earlier = jnp.where(band_col == band_row, before, 0.0) * ocean_col
    turn_row = jnp.sum(earlier, axis=0, keepdims=True)
    line = iota((lat_count * SENT, ROWS), 0)
    slot = (line // SENT * MOST + line % MOST).astype(F32)
    leaves = jnp.where(slot == band_row * 2.0 + turn_row, ocean_row, 0.0).astype(BF)
    lane = iota((ROWS, 3 * ROWS), 1)
    there = place_of(lane % ROWS).astype(F32) == order_col
    there = jnp.where(there, ocean_col, 0.0).astype(BF)
    moved = dot(leaves, there)
    line, lane = iota(moved.shape, 0), iota(moved.shape, 1)
    spread[...] = jnp.where(line % SENT // MOST == lane // ROWS, moved, 0.0).astype(BF)

    arrive = jnp.where(band_all.astype(F32) == me.astype(F32), ocean_all.astype(F32), 0.0)
    width_in = lat_count * SENT
    home = iota((LANES, width_in), 1) // SENT
    counts = dot(arrive.astype(BF), (iota((LANES, width_in), 0) // ROWS == home % 2).astype(BF))
    home = iota(counts.shape, 1) // SENT
    count_row = jnp.sum(
        jnp.where(iota(counts.shape, 0) == home // 2, counts, 0.0), axis=0, keepdims=True
    )
    sooner = jnp.where(iota(counts.shape, 0) < home // 2, counts, 0.0)
    other = dot(arrive.astype(BF), (iota((LANES, width_in), 0) // ROWS != iota((LANES, width_in), 1) // SENT % 2).astype(BF))
    sooner = sooner + jnp.where(iota(counts.shape, 0) < home // 2, other, 0.0)
    sooner = sooner + jnp.where(
        (iota(counts.shape, 0) == home // 2) & (home % 2 == 1), other, 0.0
    )
    base_row = jnp.sum(sooner, axis=0, keepdims=True)
    slots = out_ref.shape[1]
    shape = (3 * slots, width_in)
    line, lane = iota(shape, 0), iota(shape, 1)
    turn = lane % MOST
    number = (line % slots - turn).astype(F32)
    hit = (number == base_row) & (turn.astype(F32) < count_row) & (lane % SENT // MOST == line // slots)
    gather[...] = jnp.where(hit, 1.0, 0.0).astype(BF)

    bias_up, bias_one, bias_two = (
        jnp.concatenate([b[...], b[...]], axis=1) * 0.5 for b in (up_bias, first_bias, second_bias)
    )
    bias_head = jnp.concatenate([head_bias[...]] * (LANES // head_bias.shape[1]), axis=1)

    for copy in copies[:2]:
        copy.wait_recv()

    ends = iota((ROWS, SUB), 1)
    pick_ends = jnp.where(ends == 0, top, jnp.where(ends == 1, bottom, 0.0))
    pick_all = jnp.concatenate([pick.astype(BF), pick_ends.astype(BF)], axis=1)

    def two_rows(upper, lower):
        which = iota((SUB, upper.shape[1]), 0)
        return jnp.where(which == 0, upper, jnp.where(which == 1, lower, 0.0)).astype(BF)

    lifted = dot(
        pick_all, jnp.concatenate([x_ref[...], two_rows(halo[0], halo[1])], axis=0)
    ).astype(BF)
    for j in range(PAIRS):
        xc[j] = lifted[:, j * LANES : (j + 1) * LANES]
    low_lanes = iota((1, LANES), 1) < 64
    high = jnp.where(low_lanes, 0.0, 1.0).astype(BF)
    low = jnp.where(low_lanes, 1.0, 0.0).astype(BF)

    def lift(start, group):
        source = xc[pl.ds(start, group)].reshape(group * ROWS, LANES)
        z = dot(source, w_up[...])
        for a in range(3):
            for n in range(3):
                grow = gelu_of_half(z[:, (3 * a + n) * LANES :][:, :LANES] + bias_up)
                for j in range(group):
                    value = grow[j * ROWS : (j + 1) * ROWS]
                    store_layer(zero_layer, 3 * (start + j) + 1 + n, a, value, masks)

    lift(0, PAIRS // 2)
    lift(PAIRS // 2, PAIRS // 2)

    def convolve(places):
        rows = conv(zero_layer, w_pair, w_one, bias_one, 0, places)
        for a in range(3):
            for j, at in enumerate(places):
                store_layer(one_layer, at, a, rows[a][j * ROWS : (j + 1) * ROWS], masks)

    for copy in copies[2:]:
        copy.wait_recv()
    joined = jnp.where(low_lanes, side[0].astype(F32), side[1].astype(F32)).astype(BF)
    joined_ends = two_rows(
        jnp.where(low_lanes, corner[0, 0], corner[0, 1]),
        jnp.where(low_lanes, corner[1, 0], corner[1, 1]),
    )
    outer = dot(pick_all, jnp.concatenate([joined, joined_ends], axis=0)).astype(BF)
    z = dot(outer, w_up[...])
    for a in range(3):
        for n, at in ((2, 0), (0, 3 * PAIRS + 1)):
            grow = gelu_of_half(z[:, (3 * a + n) * LANES :][:, :LANES] + bias_up)
            store_layer(zero_layer, at, a, grow, masks)
    convolve(range(0, 3 * WIDE + 1))
    convolve(range(3 * WIDE + 1, 3 * PAIRS + 1))

    for half in range(2):
        base = half * 3 * WIDE
        rows = conv(one_layer, w_pair, w_one, bias_two, 1, range(base, base + 3 * WIDE))
        for a in range(3):
            for j in range(3 * WIDE):
                skip = one_layer[base + j + 1, a + 1] * low + one_layer[base + j, a + 1] * high
                grown[j, a] = rows[a][j * ROWS : (j + 1) * ROWS] + skip
        pieces = []
        for p in range(WIDE):
            made = [grown[i * WIDE + p].reshape(3 * ROWS, LANES) for i in range(3)]
            pieces.append(jnp.concatenate(made, axis=0))
        fields = dot(jnp.concatenate(pieces, axis=1), w_head[...])
        fields = (fields + bias_head).astype(BF)
        for i in range(3):
            sent = dot(spread[...], fields[i * 3 * ROWS : (i + 1) * 3 * ROWS]).astype(BF)
            outgoing[:, half * 3 + i] = sent.reshape(lat_count, 3, MOST, LANES)

    def send(t, carry):
        target = (me + t) % lat_count
        pltpu.make_async_remote_copy(
            src_ref=outgoing.at[target],
            dst_ref=incoming.at[me],
            send_sem=out_send,
            recv_sem=out_recv,
            device_id={"lat": target, "lon": lon},
            device_id_type=MESH,
        ).start()
        return carry

    lax.fori_loop(1, lat_count, send, 0)
    incoming[me] = outgoing[me]

    rest = pl.ds(0, lat_count - 1)
    pltpu.make_async_copy(incoming.at[rest], incoming.at[rest], out_recv).wait()
    for i in range(6):
        landed = incoming[:, i].reshape(lat_count * SENT, LANES)
        made = dot(gather[...], landed).astype(BF)
        for a in range(3):
            out_ref[a, :, i * LANES : (i + 1) * LANES] = made[a * slots : (a + 1) * slots]
    for copy in copies:
        copy.wait_send()
    pltpu.make_async_copy(outgoing.at[rest], outgoing.at[rest], out_send).wait()


def body(lat_count, lon_count, coarse, ocean_mask, band_plan, up_weight, up_bias, first_weight,
         first_bias, second_weight, second_bias, head_weight, head_bias):
    slots = 32
    width = coarse.shape[1]
    vmem = pl.BlockSpec(memory_space=pltpu.VMEM)
    row = lambda v: v.reshape(1, -1)
    made = pl.pallas_call(
        partial(kernel, lat_count, lon_count),
        out_shape=jax.ShapeDtypeStruct((3, slots, 768), BF),
        in_specs=[vmem] * 11,
        out_specs=vmem,
        scratch_shapes=[
            pltpu.VMEM((2, 1, width), F32),
            pltpu.VMEM((2, 1, width), F32),
            pltpu.VMEM((2, 2, 1, LANES), F32),
            pltpu.VMEM((2, ROWS, LANES), BF),
            pltpu.VMEM((PAIRS, ROWS, LANES), BF),
            pltpu.VMEM((3 * PAIRS + 2, 5, ROWS, LANES), BF),
            pltpu.VMEM((3 * PAIRS + 1, 5, ROWS, LANES), BF),
            pltpu.VMEM((3 * WIDE, 3, ROWS, LANES), BF),
            pltpu.VMEM((LANES, 9 * LANES), BF),
            pltpu.VMEM((2, 1024, 2 * LANES), BF),
            pltpu.VMEM((2, 768, LANES), BF),
            pltpu.VMEM((16 * LANES, LANES), BF),
            pltpu.VMEM((2, ROWS, LANES), BF),
            pltpu.VMEM((lat_count * SENT, 3 * ROWS), BF),
            pltpu.VMEM((3 * slots, lat_count * SENT), BF),
            pltpu.VMEM((lat_count, 6, 3, MOST, LANES), BF),
            pltpu.VMEM((lat_count, 6, 3, MOST, LANES), BF),
            pltpu.SemaphoreType.DMA((8,)),
            pltpu.SemaphoreType.DMA((8,)),
            pltpu.SemaphoreType.DMA,
            pltpu.SemaphoreType.DMA,
        ],
        compiler_params=pltpu.CompilerParams(
            collective_id=0, has_side_effects=True, vmem_limit_bytes=60 * 2**20
        ),
    )(
        coarse,
        ocean_mask.reshape(-1, LANES),
        band_plan.reshape(-1, LANES),
        up_weight,
        row(up_bias),
        first_weight,
        row(first_bias),
        second_weight,
        row(second_bias),
        head_weight.T,
        row(head_bias),
    )
    return made.transpose(1, 0, 2).astype(F32)


def solution(mesh):
    in_specs = (P("lat", "lon"), P(), P(), P(), P(), P(), P(), P(), P(), P(), P())
    out_specs = P("lat", None, "lon")
    call = partial(body, mesh.shape["lat"], mesh.shape["lon"])
    return jax.shard_map(call, mesh=mesh, in_specs=in_specs, out_specs=out_specs, check_vma=False)
```
